128 devices in a mesh: plane: 16 (over x, z), fourier: 8 (over y, core).
Axes of the slice: x: 4, y: 4, z: 4, core: 2. Of those that a mesh axis runs over, the one named last changes fastest.
Arguments:
- velocity: float32 [3, 128, 49, 128, 128], P(None, 'fourier', None, 'plane'), may hold values from -1.5 to 1.5
- metric: float32 [2, 128, 128], P(None, 'plane'), may hold values from 0.5 to 2
Outputs:
- pressure: float32 [128, 49, 128, 128], P('fourier', None, 'plane')
- residual: float32 [128, 49, 128, 128], P('fourier', None, 'plane')
The draws below stay inside these ranges and needn't reach their ends.
All inputs are finite; a program needn't handle non-finite values.
Results may differ from the reference program's by a relative error of at most 0.00065.
Values sent between devices are 32-bit elements; how exact they have to be, the bound alone decides.
No kernel may reach another device: no remote copies, remote signals or barrier semaphores. Data moves between devices by JAX's collectives and lax.ppermute only.
A program may use at most 128 MiB of HBM per device.

```python
import math
import jax
import jax.numpy as jnp
import numpy as np
from jax import lax

M = 128
NODES = 49
EI = 8
EJ = 128
NI = 128


def draw_velocity(key, part):
    key = jax.random.fold_in(key, 11)
    index = jnp.arange(M, dtype=jnp.int32)
    wavenum = jnp.where(index == 1, M // 2, index // 2).astype(jnp.float32)
    spectrum = 0.2 / (1.0 + wavenum / 8.0)
    ramp = 3.0 ** (jnp.arange(NI, dtype=jnp.float32) / (NI - 1))
    shape_all = (3, M, NODES, NI, EJ)
    base = jnp.clip(jax.random.normal(key, shape_all, jnp.float32), -2.5, 2.5)
    return base * spectrum[None, :, None, None, None] * ramp[None, None, None, :, None]


def block_levels(key, shape, pieces, low, top_value):
    gain, own = 1.0, jax.random.fold_in(key, 6)
    for position, parts in pieces:
        heights = jnp.exp(jax.random.uniform(jax.random.fold_in(own, position), (parts,), jnp.float32, low / len(pieces), top_value / len(pieces)))
        gain = gain * jnp.repeat(heights, shape[position] // parts).reshape([-1 if axis == position else 1 for axis in range(len(shape))])
    return gain


def setup_inputs(seed: int = 0) -> dict:
    arg_keys = jax.random.split(jax.random.key(seed), 3)
    velocity = draw_velocity(jax.random.fold_in(arg_keys[2], 71), 0)
    metric = jnp.clip(jnp.exp(math.log(2.0) - 1.3862944 * jax.random.uniform(arg_keys[1], (2, NI, EJ), jnp.float32) ** block_levels(arg_keys[1], (2, NI, EJ), ((1, 16),), -0.2, 0.2)), 0.5, 2.0)
    return dict(velocity=velocity, metric=metric)


PENALTY = 10.0
BETA = 0.5
MASS_REF = 0.08
HIGHEST_PRECISION = lax.Precision.HIGHEST

def node_tables():
    gll_nodes = np.array([-1.0, -0.830223896278567, -0.4688487934707142, 0.0, 0.4688487934707142, 0.830223896278567, 1.0])
    gll_weights = np.array([1.0 / 21.0, 0.2768260473615659, 0.4317453812098627, 0.4876190476190476, 0.4317453812098627, 0.2768260473615659, 1.0 / 21.0])
    identity = np.eye(7)
    differ = gll_nodes[:, None] - gll_nodes[None, :] + identity
    bary_weights = 1.0 / np.prod(differ, axis=1)
    off_diag = np.where(identity > 0.5, 0.0, bary_weights[None, :] / bary_weights[:, None] / differ)
    deriv_one = off_diag - identity * off_diag.sum(axis=1)[:, None]
    weight_diag = identity * gll_weights[None, :]
    stiff_one = deriv_one.T @ weight_diag @ deriv_one
    side_flag = np.where((np.arange(7) == 0) | (np.arange(7) == 6), 1.0, 0.0)
    rim_count = (side_flag[:, None] + side_flag[None, :]).reshape(49)
    stiff_x = np.kron(stiff_one, weight_diag)
    stiff_y = np.kron(weight_diag, stiff_one)
    system = jnp.asarray(stiff_x + stiff_y + PENALTY * np.eye(49) * rim_count[None, :], jnp.float32)
    lower = lax.linalg.cholesky(system)
    ident_big = jnp.eye(49, dtype=jnp.float32)
    half_solve = lax.linalg.triangular_solve(lower, ident_big, left_side=True, lower=True)
    block_inverse = lax.linalg.triangular_solve(lower, half_solve, left_side=True, lower=True, transpose_a=True)
    tables = (np.kron(deriv_one, identity), np.kron(identity, deriv_one), stiff_x, stiff_y, np.kron(gll_weights, gll_weights))
    return tuple((jnp.asarray(table, jnp.float32) for table in tables)) + (block_inverse,)

def mode_tables(length):
    index = np.arange(length)
    wavenum = index // 2
    wavenum[1] = length // 2
    angles = 2.0 * np.pi * np.outer(index, wavenum) / length
    use_cos = (index % 2 == 0) | (index == 1)
    basis = np.where(use_cos[None, :], np.cos(angles), np.sin(angles))
    factor = np.full(length, 2.0 / length)
    factor[:2] = 1.0 / length
    forward = factor[:, None] * basis.T
    modal_diff = np.zeros((length, length))
    even = np.arange(2, length, 2)
    modal_diff[even, even + 1] = BETA * wavenum[even]
    modal_diff[even + 1, even] = -BETA * wavenum[even]
    plane_diff = basis @ modal_diff @ forward
    wave_sq = (BETA * wavenum) ** 2
    tables = (basis, forward, modal_diff, plane_diff, wave_sq)
    return tuple((jnp.asarray(table, jnp.float32) for table in tables))

def advection(velocity, scale_x, scale_y, basis, plane_diff, diff_x, diff_y):
    physical = jnp.einsum('qc,xcnij->xqnij', basis, velocity, precision=HIGHEST_PRECISION)
    along_z = jnp.einsum('qp,xpnij->xqnij', plane_diff, physical, precision=HIGHEST_PRECISION)
    along_x = jnp.einsum('mn,xqnij->xqmij', diff_x, physical, precision=HIGHEST_PRECISION) * scale_x
    along_y = jnp.einsum('mn,xqnij->xqmij', diff_y, physical, precision=HIGHEST_PRECISION) * scale_y
    return physical[0] * along_x + physical[1] * along_y + physical[2] * along_z

def divergence_physical(advect, scale_x, scale_y, plane_diff, diff_x, diff_y):
    part_x = jnp.einsum('mn,qnij->qmij', diff_x, advect[0], precision=HIGHEST_PRECISION)
    part_y = jnp.einsum('mn,qnij->qmij', diff_y, advect[1], precision=HIGHEST_PRECISION)
    part_z = jnp.einsum('qp,pnij->qnij', plane_diff, advect[2], precision=HIGHEST_PRECISION)
    return scale_x * part_x + scale_y * part_y + part_z

def apply_operator(field, west_row, east_row, scale_x, scale_y, wave_sq, stiff_x, stiff_y, masses):
    ratio = scale_x / scale_y
    stiffness = ratio * jnp.einsum('mn,cnij->cmij', stiff_x, field, precision=HIGHEST_PRECISION)
    stiffness = stiffness + jnp.einsum('mn,cnij->cmij', stiff_y, field, precision=HIGHEST_PRECISION) / ratio
    stiffness = stiffness + wave_sq[:, None, None, None] * masses[None, :, None, None] / (scale_x * scale_y) * field
    lattice = field.reshape(field.shape[0], 7, 7, field.shape[2], field.shape[3])
    jumps = jnp.zeros_like(lattice)
    jumps = jumps.at[:, 0].add(lattice[:, 0] - west_row).at[:, 6].add(lattice[:, 6] - east_row)
    south_row = jnp.pad(lattice[:, :, 6], ((0, 0), (0, 0), (0, 0), (1, 0)))[..., :-1]
    north_row = jnp.pad(lattice[:, :, 0], ((0, 0), (0, 0), (0, 0), (0, 1)))[..., 1:]
    jumps = jumps.at[:, :, 0].add(lattice[:, :, 0] - south_row).at[:, :, 6].add(lattice[:, :, 6] - north_row)
    return stiffness + PENALTY * jumps.reshape(field.shape)

def precondition(resid, scale_x, scale_y, wave_sq, block_inverse):
    divisor = 0.5 * (scale_x / scale_y + scale_y / scale_x) + wave_sq[:, None, None] * MASS_REF / (scale_x * scale_y)
    return jnp.einsum('mn,cnij->cmij', block_inverse, resid, precision=HIGHEST_PRECISION) / divisor[:, None]

def inner(left, right):
    return jnp.sum(left * right, axis=(1, 2, 3))

def reference(velocity, metric):
    diff_x, diff_y, stiff_x, stiff_y, masses, block_inverse = node_tables()
    basis, forward, modal_diff, plane_diff, wave_sq = mode_tables(M)
    scale_x = metric[0]
    scale_y = metric[1]

    def forcing(block):
        start = block * EI
        vel_block = lax.dynamic_slice_in_dim(velocity, start, EI, 3)
        met_block = lax.dynamic_slice_in_dim(metric, start, EI, 1)
        advect = advection(vel_block, met_block[0], met_block[1], basis, plane_diff, diff_x, diff_y)
        div_phys = divergence_physical(advect, met_block[0], met_block[1], plane_diff, diff_x, diff_y)
        spectral = jnp.einsum('cq,qnij->cnij', forward, div_phys, precision=HIGHEST_PRECISION)
        return -(masses[:, None, None] / (met_block[0] * met_block[1])) * spectral
    blocks = lax.map(forcing, jnp.arange(NI // EI, dtype=jnp.int32))
    source = jnp.moveaxis(blocks, 0, 2).reshape(M, NODES, NI, EJ)

    def operate(field, wave_one):
        lattice = field.reshape(1, 7, 7, NI, EJ)
        west_row = jnp.pad(lattice[:, 6], ((0, 0), (0, 0), (1, 0), (0, 0)))[:, :, :-1]
        east_row = jnp.pad(lattice[:, 0], ((0, 0), (0, 0), (0, 1), (0, 0)))[:, :, 1:]
        return apply_operator(field, west_row, east_row, scale_x, scale_y, wave_one, stiff_x, stiff_y, masses)

    def solve_mode(pair):
        plane_source, wave_value = pair
        wave_one = wave_value.reshape(1)
        resid = plane_source[None]
        search_a = precondition(resid, scale_x, scale_y, wave_one, block_inverse)
        image_a = operate(search_a, wave_one)
        norm_a = inner(image_a, image_a)
        step_a = inner(resid, image_a) / norm_a
        solution = step_a[:, None, None, None] * search_a
        resid = resid - step_a[:, None, None, None] * image_a
        search_b = precondition(resid, scale_x, scale_y, wave_one, block_inverse)
        image_b = operate(search_b, wave_one)
        proj_coef = inner(image_b, image_a) / norm_a
        search_b = search_b - proj_coef[:, None, None, None] * search_a
        image_b = image_b - proj_coef[:, None, None, None] * image_a
        step_b = inner(resid, image_b) / inner(image_b, image_b)
        solution = solution + step_b[:, None, None, None] * search_b
        resid = resid - step_b[:, None, None, None] * image_b
        return (solution[0], resid[0])
    pressure, residual = lax.map(solve_mode, (source, wave_sq))
    return (pressure, residual)
```

```python
import functools

import jax
import jax.numpy as jnp
import numpy as np
from jax import lax
from jax.experimental import pallas as pl
from jax.experimental.pallas import tpu as pltpu
from jax.sharding import PartitionSpec as P

PENALTY = 10.0
BETA = 0.5
MASS_REF = 0.08
LANES = 128
F32 = jnp.float32
BF16 = jnp.bfloat16
MIB = 1 << 20


def node_tables():
    nodes = np.array(
        [
            -1.0,
            -0.830223896278567,
            -0.4688487934707142,
            0.0,
            0.4688487934707142,
            0.830223896278567,
            1.0,
        ]
    )
    weights = np.array(
        [
            1.0 / 21.0,
            0.2768260473615659,
            0.4317453812098627,
            0.4876190476190476,
            0.4317453812098627,
            0.2768260473615659,
            1.0 / 21.0,
        ]
    )
    identity = np.eye(7)
    differ = nodes[:, None] - nodes[None, :] + identity
    bary = 1.0 / np.prod(differ, axis=1)
    off_diag = np.where(identity > 0.5, 0.0, bary[None, :] / bary[:, None] / differ)
    deriv = off_diag - identity * off_diag.sum(axis=1)[:, None]
    weight_diag = identity * weights[None, :]
    stiff = deriv.T @ weight_diag @ deriv
    side = np.where((np.arange(7) == 0) | (np.arange(7) == 6), 1.0, 0.0)
    rim = (side[:, None] + side[None, :]).reshape(49)
    system = np.kron(stiff, weight_diag) + np.kron(weight_diag, stiff)
    system = system + PENALTY * np.eye(49) * rim[None, :]
    system = system.astype(np.float32).astype(np.float64)
    return weights, deriv, stiff, np.linalg.inv(system)


def mode_tables(length):
    index = np.arange(length)
    wavenum = index // 2
    wavenum[1] = length // 2
    angles = 2.0 * np.pi * np.outer(index, wavenum) / length
    use_cos = (index % 2 == 0) | (index == 1)
    basis = np.where(use_cos[None, :], np.cos(angles), np.sin(angles))
    factor = np.full(length, 2.0 / length)
    factor[:2] = 1.0 / length
    forward = factor[:, None] * basis.T
    modal_diff = np.zeros((length, length))
    even = np.arange(2, length, 2)
    modal_diff[even, even + 1] = BETA * wavenum[even]
    modal_diff[even + 1, even] = -BETA * wavenum[even]
    wave_sq = (BETA * wavenum) ** 2
    return basis, forward, modal_diff, wave_sq


WEIGHTS, DERIV, STIFF, BLOCK_INV = node_tables()

ANALYSIS = np.zeros((7, 7))
SYNTHESIS = np.zeros((7, 7))
for _k in range(3):
    ANALYSIS[_k, _k] = ANALYSIS[_k, 6 - _k] = 1.0
    ANALYSIS[4 + _k, _k] = 1.0
    ANALYSIS[4 + _k, 6 - _k] = -1.0
    SYNTHESIS[_k, _k] = SYNTHESIS[6 - _k, _k] = 1.0
    SYNTHESIS[_k, 4 + _k] = 1.0
    SYNTHESIS[6 - _k, 4 + _k] = -1.0
ANALYSIS[3, 3] = SYNTHESIS[3, 3] = 1.0


def parity_form(matrix):
    return np.linalg.inv(SYNTHESIS) @ matrix @ np.linalg.inv(ANALYSIS)


DERIV_P = parity_form(DERIV)
STIFF_P = parity_form(STIFF)
_S2 = np.kron(ANALYSIS, ANALYSIS)
_R2 = np.kron(SYNTHESIS, SYNTHESIS)
BLOCK_P = np.linalg.inv(_R2) @ BLOCK_INV @ np.linalg.inv(_S2)
BLOCK_P = BLOCK_P.reshape(7, 7, 7, 7)


def analyse(v):
    return [v[0] + v[6], v[1] + v[5], v[2] + v[4], v[3], v[0] - v[6], v[1] - v[5], v[2] - v[4]]


def synthesise(g):
    return [
        g[0] + g[4],
        g[1] + g[5],
        g[2] + g[6],
        g[3],
        g[2] - g[6],
        g[1] - g[5],
        g[0] - g[4],
    ]


def mat_rows(matrix, v):
    out = []
    for row in matrix:
        acc = None
        for coef, item in zip(row, v):
            if abs(coef) > 1e-11:
                term = item * np.float32(coef)
                acc = term if acc is None else acc + term
        out.append(acc)
    return out


def derive(v):
    g = analyse(v)
    even = mat_rows(DERIV_P[:4, 4:], g[4:])
    odd = mat_rows(DERIV_P[4:, :4], g[:4])
    out = [even[k] + odd[k] for k in range(3)]
    return out + [even[3]] + [even[k] - odd[k] for k in (2, 1, 0)]


def stiffen(v):
    g = analyse(v)
    return synthesise(mat_rows(STIFF_P[:4, :4], g[:4]) + mat_rows(STIFF_P[4:, 4:], g[4:]))


def symmetric_sector(table, x, size):
    pairs = [(i, j) for i in range(size) for j in range(i, size)]
    anti = [(i, j) for i in range(size) for j in range(i + 1, size)]
    plus = [x[i][j] if i == j else x[i][j] + x[j][i] for i, j in pairs]
    minus = [x[i][j] - x[j][i] for i, j in anti]

    def sym_row(i, j):
        return [0.5 * (table[i, j, k, l] + table[i, j, l, k]) for k, l in pairs]

    def anti_row(i, j):
        return [0.5 * (table[i, j, k, l] - table[i, j, l, k]) for k, l in anti]

    top = dict(zip(pairs, mat_rows([sym_row(i, j) for i, j in pairs], plus)))
    low = dict(zip(anti, mat_rows([anti_row(i, j) for i, j in anti], minus)))
    out = [[None] * size for _ in range(size)]
    for i, j in pairs:
        if i == j:
            out[i][j] = top[i, j]
        else:
            out[i][j] = top[i, j] + low[i, j]
            out[j][i] = top[i, j] - low[i, j]
    return out


def block_solve(v):
    part = [[None] * 7 for _ in range(7)]
    for b in range(7):
        column = analyse([v[7 * a + b] for a in range(7)])
        for k in range(7):
            part[k][b] = column[k]
    part = [analyse(part[k]) for k in range(7)]
    out = [[None] * 7 for _ in range(7)]
    ev, od = slice(0, 4), slice(4, 7)
    for rows, cols in ((ev, ev), (od, od), (ev, od), (od, ev)):
        ri, ci = range(7)[rows], range(7)[cols]
        x = [[part[i][j] for j in ci] for i in ri]
        table = BLOCK_P[rows, cols, rows, cols]
        if rows == cols:
            y = symmetric_sector(table, x, len(ri))
        else:
            n = len(ri) * len(ci)
            flat = mat_rows(table.reshape(n, n), [x[i][j] for i in range(len(ri)) for j in range(len(ci))])
            y = [flat[i * len(ci) : (i + 1) * len(ci)] for i in range(len(ri))]
        for i, row in zip(ri, y):
            for j, item in zip(ci, row):
                out[i][j] = item
    out = [synthesise(out[k]) for k in range(7)]
    res = [None] * 49
    for b in range(7):
        column = synthesise([out[k][b] for k in range(7)])
        for a in range(7):
            res[7 * a + b] = column[a]
    return res


def params(limit_mib, grid=None):
    semantics = None if grid is None else ("arbitrary",) * grid
    return pltpu.CompilerParams(vmem_limit_bytes=limit_mib * MIB, dimension_semantics=semantics)


def pack_kernel(in_ref, out_ref):
    def step(n, carry):
        for i in range(8):
            out_ref[i, 0, n] = in_ref[pl.ds(n * 8 + i, 8, stride=392), :]
        return carry

    lax.fori_loop(0, 49, step, 0, unroll=7)


def pack(velocity):
    flat = velocity.reshape(3 * 16 * 392, LANES)
    return pl.pallas_call(
        pack_kernel,
        grid=(3, 2),
        in_specs=[pl.BlockSpec((8 * 392, LANES), lambda x, h: (2 * x + h, 0))],
        out_specs=pl.BlockSpec((8, 1, 49, 8, LANES), lambda x, h: (0, x, 0, h, 0)),
        out_shape=jax.ShapeDtypeStruct((8, 3, 49, 16, LANES), F32),
        compiler_params=params(32, 2),
        name="pack",
    )(flat)


def forcing_kernel(in_ref, met_ref, wp_ref, wl_ref, fh_ref, fl_ref, out_ref, xb, u, z, adv, div):
    a = pl.program_id(0)
    sx = met_ref[0]
    sy = met_ref[1]
    for x in range(3):
        for b in range(7):
            block = in_ref[:, x, b].reshape(128, LANES)
            hi = block.astype(BF16)
            lo = (block - hi.astype(F32)).astype(BF16)
            xb[0:128, b * 128 : b * 128 + 128] = hi
            xb[128:256, b * 128 : b * 128 + 128] = lo
        both = jnp.dot(wp_ref[...], xb[...], preferred_element_type=F32)
        both = both + jnp.dot(wl_ref[...], xb[0:128], preferred_element_type=F32)
        u[x, a] = both[0:128]
        z[x] = both[128:256]

    def along_b(t, carry):
        q = pl.ds(pl.multiple_of(t * 8, 8), 8)
        lanes = [pl.ds(b * 128, 128) for b in range(7)]
        fields = [[u[i, a, q, s] for s in lanes] for i in range(3)]
        scaled = [item * sy for item in fields[1]]
        for i in range(3):
            slope = derive(fields[i])
            for b in range(7):
                adv[i, a, q, lanes[b]] = scaled[b] * slope[b] + fields[2][b] * z[i, q, lanes[b]]
        return carry

    lax.fori_loop(0, 16, along_b, 0)

    @pl.when(a == 6)
    def _():
        def along_a(t, carry):
            q = pl.ds(pl.multiple_of(t * 8, 8), 8)
            q2 = pl.ds(pl.multiple_of(t * 8 + 128, 8), 8)
            for b in range(7):
                s = pl.ds(b * 128, 128)
                first = [u[0, k, q, s] for k in range(7)]
                scaled = [item * sx for item in first]
                for i in range(3):
                    slope = derive(first if i == 0 else [u[i, k, q, s] for k in range(7)])
                    total = [scaled[k] * slope[k] + adv[i, k, q, s] for k in range(7)]
                    if i == 0:
                        total = [item * sx for item in derive(total)]
                    for k in range(7):
                        if i == 0:
                            div[k, q, s] = total[k]
                        elif i == 1:
                            adv[1, k, q, s] = total[k]
                        else:
                            div[k, q2, s] = total[k]
            for k in range(7):
                slope = derive([adv[1, k, q, pl.ds(b * 128, 128)] for b in range(7)])
                for b in range(7):
                    s = pl.ds(b * 128, 128)
                    div[k, q, s] = div[k, q, s] + sy * slope[b]
            return carry

        lax.fori_loop(0, 16, along_a, 0)
        area = -1.0 / (sx * sy)
        for k in range(7):
            block = div[k]
            hi = block.astype(BF16)
            lo = (block - hi.astype(F32)).astype(BF16)
            spec = jnp.dot(fh_ref[...], hi, preferred_element_type=F32)
            spec = spec + jnp.dot(fh_ref[...], lo, preferred_element_type=F32)
            spec = spec + jnp.dot(fl_ref[...], hi, preferred_element_type=F32)
            for b in range(7):
                scale = area * np.float32(WEIGHTS[k] * WEIGHTS[b])
                out_ref[:, 7 * k + b] = (spec[:, b * 128 : b * 128 + 128] * scale).reshape(8, 16, LANES)


def split_bf16(table):
    table = jnp.asarray(table, F32)
    hi = table.astype(BF16)
    return hi, (table - hi.astype(F32)).astype(BF16)


def forcing(gathered, met_row, basis, forward, modal_diff):
    both = np.concatenate([basis, basis @ modal_diff], axis=0)
    back = np.concatenate([forward, modal_diff @ forward], axis=1)
    wh, wl = split_bf16(both)
    fh, fl = split_bf16(back)
    wp = jnp.concatenate([wh, wh], axis=1)

    def whole(shape):
        return pl.BlockSpec(shape, lambda a: (0,) * len(shape))

    return pl.pallas_call(
        forcing_kernel,
        grid=(7,),
        in_specs=[
            pl.BlockSpec((8, 3, 7, 16, LANES), lambda a: (0, 0, a, 0, 0)),
            whole((2, 1, LANES)),
            whole((256, 256)),
            whole((256, 128)),
            whole((128, 256)),
            whole((128, 256)),
        ],
        out_specs=whole((8, 49, 16, LANES)),
        out_shape=jax.ShapeDtypeStruct((8, 49, 16, LANES), F32),
        scratch_shapes=[
            pltpu.VMEM((256, 896), BF16),
            pltpu.VMEM((3, 7, 128, 896), F32),
            pltpu.VMEM((3, 128, 896), F32),
            pltpu.VMEM((3, 7, 128, 896), F32),
            pltpu.VMEM((7, 256, 896), F32),
        ],
        compiler_params=params(56, 1),
        name="forcing",
    )(gathered, met_row, wp, wl, fh, fl)


def rows_of(c, n):
    return pl.ds(pl.multiple_of(c * 392 + n * 8, 8), 8)


def metric_values(met_ref):
    sx, sy = met_ref[0], met_ref[1]
    ratio = sx / sy
    back = sy / sx
    return ratio, back, 1.0 / (sx * sy)


def inverse_divisor(ratio, back, area, wave):
    return 1.0 / (0.5 * (ratio + back) + (wave * MASS_REF) * area)


def store_rims(field, c, east_ref, west_ref):
    for b in range(7):
        east_ref[pl.ds(c * 8 + b, 1), :] = field[42 + b][7:8]
        west_ref[pl.ds(c * 8 + b, 1), :] = field[b][0:1]


def apply_operator(v, c, wave, ratio, back, area, west_ref, east_ref):
    kind = [0, 1, 2, 3, 2, 1, 0]
    sub = lax.broadcasted_iota(jnp.int32, (8, LANES), 0)
    lane = lax.broadcasted_iota(jnp.int32, (8, LANES), 1)
    w = [np.float32(WEIGHTS[k]) for k in range(4)]
    ratio_w = [ratio * w[k] for k in range(4)]
    back_w = [back * w[k] for k in range(4)]
    mass = wave * area
    diag = {}
    for i in range(4):
        for j in range(i, 4):
            rim = PENALTY * ((i == 0) + (j == 0))
            diag[i, j] = mass * np.float32(WEIGHTS[i] * WEIGHTS[j]) + np.float32(rim)
    out = [None] * 49
    for b in range(7):
        column = stiffen([v[7 * a + b] for a in range(7)])
        for a in range(7):
            key = tuple(sorted((kind[a], kind[b])))
            out[7 * a + b] = column[a] * ratio_w[kind[b]] + v[7 * a + b] * diag[key]
    for a in range(7):
        line = stiffen([v[7 * a + b] for b in range(7)])
        for b in range(7):
            out[7 * a + b] = out[7 * a + b] + line[b] * back_w[kind[a]]
    ten = np.float32(PENALTY)
    for b in range(7):
        west = west_ref[pl.ds(c * 8 + b, 1), :]
        east = east_ref[pl.ds(c * 8 + b, 1), :]
        before = jnp.where(sub == 0, west, pltpu.roll(v[42 + b], 1, 0))
        after = jnp.where(sub == 7, east, pltpu.roll(v[b], 7, 0))
        out[b] = out[b] - ten * before
        out[42 + b] = out[42 + b] - ten * after
    for a in range(7):
        south = jnp.where(lane == 0, 0.0, pltpu.roll(v[7 * a + 6], 1, 1))
        north = jnp.where(lane == 127, 0.0, pltpu.roll(v[7 * a], 127, 1))
        out[7 * a] = out[7 * a] - ten * south
        out[7 * a + 6] = out[7 * a + 6] - ten * north
    return out


def first_kernel(wave_ref, recv_ref, met_ref, r_ref, p_ref, east_ref, west_ref):
    def unpack(n, carry):
        for i in range(8):
            r_ref[pl.ds(n * 8 + i, 16, stride=392), :] = recv_ref[i, n]
        return carry

    lax.fori_loop(0, 49, unpack, 0, unroll=7)
    east_ref[...] = jnp.zeros_like(east_ref)
    west_ref[...] = jnp.zeros_like(west_ref)
    ratio, back, area = metric_values(met_ref)

    def step(c, carry):
        inv = inverse_divisor(ratio, back, area, wave_ref[c])
        field = block_solve([r_ref[rows_of(c, n), :] for n in range(49)])
        field = [item * inv for item in field]
        for n in range(49):
            p_ref[rows_of(c, n), :] = field[n]
        store_rims(field, c, east_ref, west_ref)
        return carry

    lax.fori_loop(0, 16, step, 0)


def second_kernel(
    wave_ref, p_ref, met_ref, west_in, east_in, q_ref, s_ref, east_ref, west_ref
):
    east_ref[...] = jnp.zeros_like(east_ref)
    west_ref[...] = jnp.zeros_like(west_ref)
    ratio, back, area = metric_values(met_ref)

    def image(c, carry):
        v = [p_ref[rows_of(c, n), :] for n in range(49)]
        out = apply_operator(v, c, wave_ref[c], ratio, back, area, west_in, east_in)
        for n in range(49):
            q_ref[rows_of(c, n), :] = out[n]
        return carry

    lax.fori_loop(0, 16, image, 0)

    def search(c, carry):
        inv = inverse_divisor(ratio, back, area, wave_ref[c])
        field = block_solve([q_ref[rows_of(c, n), :] for n in range(49)])
        field = [item * inv for item in field]
        for n in range(49):
            s_ref[rows_of(c, n), :] = field[n]
        store_rims(field, c, east_ref, west_ref)
        return carry

    lax.fori_loop(0, 16, search, 0)


def third_kernel(
    wave_ref, r_ref, q_ref, s_ref, met_ref, west_in, east_in, t_ref, dots_ref, acc_ref
):
    ratio, back, area = metric_values(met_ref)

    def image(c, carry):
        v = [s_ref[rows_of(c, n), :] for n in range(49)]
        out = apply_operator(v, c, wave_ref[c], ratio, back, area, west_in, east_in)
        sums = [None] * 5
        for n in range(49):
            t_ref[rows_of(c, n), :] = out[n]
            q, r, t = q_ref[rows_of(c, n), :], r_ref[rows_of(c, n), :], out[n]
            for k, term in enumerate((q * q, r * q, t * q, t * t, r * t)):
                sums[k] = term if sums[k] is None else sums[k] + term
        for k in range(5):
            acc_ref[k, pl.ds(c, 1), :] = jnp.sum(sums[k], axis=0, keepdims=True)
        return carry

    lax.fori_loop(0, 16, image, 0)
    lane = lax.broadcasted_iota(jnp.int32, (16, LANES), 1)
    table = jnp.zeros((16, LANES), F32)
    for k in range(5):
        table = jnp.where(lane == k, jnp.sum(acc_ref[k], axis=1, keepdims=True), table)
    for d in range(16):
        dots_ref[d] = table


def last_kernel(dots_ref, r_ref, p_ref, q_ref, s_ref, t_ref, pres_ref, resid_ref, coef_ref):
    total = dots_ref[0]
    for d in range(1, 16):
        total = total + dots_ref[d]
    lane = lax.broadcasted_iota(jnp.int32, (16, LANES), 1)

    def pick(k):
        return jnp.sum(jnp.where(lane == k, total, 0.0), axis=1, keepdims=True)

    qq, rq, tq, tt, rt = [pick(k) for k in range(5)]
    alpha = rq / qq
    gamma = tq / qq
    lam = (rt - gamma * rq) / (tt - gamma * tq)
    coef_ref[0] = jnp.broadcast_to(alpha - lam * gamma, (16, LANES))
    coef_ref[1] = jnp.broadcast_to(lam, (16, LANES))

    def step(c, carry):
        first = coef_ref[0, pl.ds(c, 1), :]
        second = coef_ref[1, pl.ds(c, 1), :]
        for n in range(49):
            at = rows_of(c, n)
            pres_ref[at, :] = first * p_ref[at, :] + second * s_ref[at, :]
            resid_ref[at, :] = r_ref[at, :] - first * q_ref[at, :] - second * t_ref[at, :]
        return carry

    lax.fori_loop(0, 16, step, 0)


FIELD = (16 * 392, LANES)
RIM = (16 * 8, LANES)


def call(kernel, name, inputs, smem, outs, limit, scratch=()):
    specs = [
        pl.BlockSpec(memory_space=pltpu.SMEM if i in smem else pltpu.VMEM)
        for i in range(len(inputs))
    ]
    return pl.pallas_call(
        kernel,
        in_specs=specs,
        out_specs=tuple(pl.BlockSpec(memory_space=pltpu.VMEM) for _ in outs),
        out_shape=tuple(jax.ShapeDtypeStruct(s, F32) for s in outs),
        scratch_shapes=list(scratch),
        compiler_params=params(limit),
        name=name,
    )(*inputs)


def body(velocity, metric):
    modes_here = velocity.shape[1]
    basis, forward, modal_diff, wave_all = mode_tables(modes_here * lax.axis_size("fourier"))
    mine = lax.axis_index("fourier")
    wave = lax.dynamic_slice_in_dim(jnp.asarray(wave_all, F32), mine * modes_here, modes_here)
    met_row = lax.dynamic_slice_in_dim(metric, mine, 1, 1)

    packed = pack(velocity)
    gathered = lax.all_to_all(packed, "fourier", 0, 0, tiled=True)
    source = forcing(gathered, met_row, basis, forward, modal_diff)
    recv = lax.all_to_all(source, "fourier", 0, 0, tiled=True)

    size = lax.axis_size("plane")
    up = [(i, i + 1) for i in range(size - 1)]
    down = [(j, i) for i, j in up]

    def exchange(east, west):
        return lax.ppermute(east, "plane", up), lax.ppermute(west, "plane", down)

    r, p1, east, west = call(
        first_kernel, "first", (wave, recv, metric), (0,), (FIELD, FIELD, RIM, RIM), 40
    )
    west_in, east_in = exchange(east, west)
    q1, s, east, west = call(
        second_kernel,
        "second",
        (wave, p1, metric, west_in, east_in),
        (0,),
        (FIELD, FIELD, RIM, RIM),
        40,
    )
    west_in, east_in = exchange(east, west)
    t, dots = call(
        third_kernel,
        "third",
        (wave, r, q1, s, metric, west_in, east_in),
        (0,),
        (FIELD, (16, 16, LANES)),
        40,
        [pltpu.VMEM((5, 16, LANES), F32)],
    )
    dots = lax.all_to_all(dots, "plane", 0, 0, tiled=True)
    pressure, residual = call(
        last_kernel,
        "last",
        (dots, r, p1, q1, s, t),
        (),
        (FIELD, FIELD),
        40,
        [pltpu.VMEM((2, 16, LANES), F32)],
    )
    shape = velocity.shape[1:]
    return pressure.reshape(shape), residual.reshape(shape)


def solution(mesh):
    in_specs = (P(None, "fourier", None, "plane", None), P(None, "plane", None))
    out_specs = (P("fourier", None, "plane", None), P("fourier", None, "plane", None))
    return jax.shard_map(body, mesh=mesh, in_specs=in_specs, out_specs=out_specs, check_vma=False)
```

```python
import jax
import jax.numpy as jnp
import ml_dtypes
import numpy as np
from jax import lax
from jax.experimental import pallas as pl
from jax.experimental.pallas import tpu as pltpu
from jax.sharding import PartitionSpec as P

PENALTY = 10.0
BETA = 0.5
MASS_REF = 0.08
LANES = 128
F32 = jnp.float32
BF16 = jnp.bfloat16
MIB = 1 << 20
FULL = 60


def node_tables():
    nodes = np.array(
        [
            -1.0,
            -0.830223896278567,
            -0.4688487934707142,
            0.0,
            0.4688487934707142,
            0.830223896278567,
            1.0,
        ]
    )
    weights = np.array(
        [
            1.0 / 21.0,
            0.2768260473615659,
            0.4317453812098627,
            0.4876190476190476,
            0.4317453812098627,
            0.2768260473615659,
            1.0 / 21.0,
        ]
    )
    identity = np.eye(7)
    differ = nodes[:, None] - nodes[None, :] + identity
    bary = 1.0 / np.prod(differ, axis=1)
    off_diag = np.where(identity > 0.5, 0.0, bary[None, :] / bary[:, None] / differ)
    deriv = off_diag - identity * off_diag.sum(axis=1)[:, None]
    weight_diag = identity * weights[None, :]
    stiff = deriv.T @ weight_diag @ deriv
    side = np.where((np.arange(7) == 0) | (np.arange(7) == 6), 1.0, 0.0)
    rim = (side[:, None] + side[None, :]).reshape(49)
    system = np.kron(stiff, weight_diag) + np.kron(weight_diag, stiff)
    system = system + PENALTY * np.eye(49) * rim[None, :]
    system = system.astype(np.float32).astype(np.float64)
    return weights, deriv, stiff, np.linalg.inv(system)


def mode_tables(length):
    index = np.arange(length)
    wavenum = index // 2
    wavenum[1] = length // 2
    angles = 2.0 * np.pi * np.outer(index, wavenum) / length
    use_cos = (index % 2 == 0) | (index == 1)
    basis = np.where(use_cos[None, :], np.cos(angles), np.sin(angles))
    factor = np.full(length, 2.0 / length)
    factor[:2] = 1.0 / length
    forward = factor[:, None] * basis.T
    modal_diff = np.zeros((length, length))
    even = np.arange(2, length, 2)
    modal_diff[even, even + 1] = BETA * wavenum[even]
    modal_diff[even + 1, even] = -BETA * wavenum[even]
    wave_sq = (BETA * wavenum) ** 2
    return basis, forward, modal_diff, wave_sq


WEIGHTS, DERIV, STIFF, BLOCK_INV = node_tables()

ANALYSIS = np.zeros((7, 7))
SYNTHESIS = np.zeros((7, 7))
for _k in range(3):
    ANALYSIS[_k, _k] = ANALYSIS[_k, 6 - _k] = 1.0
    ANALYSIS[4 + _k, _k] = 1.0
    ANALYSIS[4 + _k, 6 - _k] = -1.0
    SYNTHESIS[_k, _k] = SYNTHESIS[6 - _k, _k] = 1.0
    SYNTHESIS[_k, 4 + _k] = 1.0
    SYNTHESIS[6 - _k, 4 + _k] = -1.0
ANALYSIS[3, 3] = SYNTHESIS[3, 3] = 1.0


def parity_form(matrix):
    return np.linalg.inv(SYNTHESIS) @ matrix @ np.linalg.inv(ANALYSIS)


DERIV_P = parity_form(DERIV)
STIFF_P = parity_form(STIFF)
_S2 = np.kron(ANALYSIS, ANALYSIS)
_R2 = np.kron(SYNTHESIS, SYNTHESIS)
BLOCK_P = np.linalg.inv(_R2) @ BLOCK_INV @ np.linalg.inv(_S2)
BLOCK_P = BLOCK_P.reshape(7, 7, 7, 7)


def analyse(v):
    return [v[0] + v[6], v[1] + v[5], v[2] + v[4], v[3], v[0] - v[6], v[1] - v[5], v[2] - v[4]]


def synthesise(g):
    return [
        g[0] + g[4],
        g[1] + g[5],
        g[2] + g[6],
        g[3],
        g[2] - g[6],
        g[1] - g[5],
        g[0] - g[4],
    ]


def mat_rows(matrix, v):
    out = []
    for row in matrix:
        acc = None
        for coef, item in zip(row, v):
            if abs(coef) > 1e-11:
                term = item * np.float32(coef)
                acc = term if acc is None else acc + term
        out.append(acc)
    return out


def derive(v):
    g = analyse(v)
    even = mat_rows(DERIV_P[:4, 4:], g[4:])
    odd = mat_rows(DERIV_P[4:, :4], g[:4])
    out = [even[k] + odd[k] for k in range(3)]
    return out + [even[3]] + [even[k] - odd[k] for k in (2, 1, 0)]


def stiffen(v):
    g = analyse(v)
    return synthesise(mat_rows(STIFF_P[:4, :4], g[:4]) + mat_rows(STIFF_P[4:, 4:], g[4:]))


def symmetric_sector(table, x, size):
    pairs = [(i, j) for i in range(size) for j in range(i, size)]
    anti = [(i, j) for i in range(size) for j in range(i + 1, size)]
    plus = [x[i][j] if i == j else x[i][j] + x[j][i] for i, j in pairs]
    minus = [x[i][j] - x[j][i] for i, j in anti]

    def sym_row(i, j):
        return [0.5 * (table[i, j, k, l] + table[i, j, l, k]) for k, l in pairs]

    def anti_row(i, j):
        return [0.5 * (table[i, j, k, l] - table[i, j, l, k]) for k, l in anti]

    top = dict(zip(pairs, mat_rows([sym_row(i, j) for i, j in pairs], plus)))
    low = dict(zip(anti, mat_rows([anti_row(i, j) for i, j in anti], minus)))
    out = [[None] * size for _ in range(size)]
    for i, j in pairs:
        if i == j:
            out[i][j] = top[i, j]
        else:
            out[i][j] = top[i, j] + low[i, j]
            out[j][i] = top[i, j] - low[i, j]
    return out


def block_solve(v):
    part = [[None] * 7 for _ in range(7)]
    for b in range(7):
        column = analyse([v[7 * a + b] for a in range(7)])
        for k in range(7):
            part[k][b] = column[k]
    part = [analyse(part[k]) for k in range(7)]
    out = [[None] * 7 for _ in range(7)]
    ev, od = slice(0, 4), slice(4, 7)
    for rows, cols in ((ev, ev), (od, od), (ev, od), (od, ev)):
        ri, ci = range(7)[rows], range(7)[cols]
        x = [[part[i][j] for j in ci] for i in ri]
        table = BLOCK_P[rows, cols, rows, cols]
        if rows == cols:
            y = symmetric_sector(table, x, len(ri))
        else:
            n = len(ri) * len(ci)
            flat = mat_rows(table.reshape(n, n), [x[i][j] for i in range(len(ri)) for j in range(len(ci))])
            y = [flat[i * len(ci) : (i + 1) * len(ci)] for i in range(len(ri))]
        for i, row in zip(ri, y):
            for j, item in zip(ci, row):
                out[i][j] = item
    out = [synthesise(out[k]) for k in range(7)]
    res = [None] * 49
    for b in range(7):
        column = synthesise([out[k][b] for k in range(7)])
        for a in range(7):
            res[7 * a + b] = column[a]
    return res


def params(limit_mib, grid=None):
    semantics = None if grid is None else ("arbitrary",) * grid
    return pltpu.CompilerParams(vmem_limit_bytes=limit_mib * MIB, dimension_semantics=semantics)


STEPS = ((0, 0), (1, 0), (3, 0), (2, 0), (1, 1), (3, 1), (2, 1), (0, 1))


def partner(me, d, flip):
    core = me % 2
    return ((me // 2 + d) % 4) * 2 + (core + flip - 2 * core * flip)


def permute(value, step):
    d, flip = STEPS[step]
    return lax.ppermute(value, "fourier", [(i, partner(i, d, flip)) for i in range(8)])


def target(me, step):
    return partner(me, *STEPS[step])


def origin(me, step):
    d, flip = STEPS[step]
    return partner(me, (4 - d) % 4, flip)


def pack_kernel(me_ref, in_ref, *out_refs):
    me = me_ref[0]
    rows = [target(me, s) for s in range(8)]

    def step(n, carry):
        for s in range(8):
            out_refs[s][n] = in_ref[pl.ds(n * 8 + rows[s], 8, stride=392), :]
        return carry

    lax.fori_loop(0, 49, step, 0, unroll=7)


def pack(me, flat, x):
    return pl.pallas_call(
        pack_kernel,
        grid=(2,),
        in_specs=[
            pl.BlockSpec(memory_space=pltpu.SMEM),
            pl.BlockSpec((8 * 392, LANES), lambda h: (2 * x + h, 0)),
        ],
        out_specs=[pl.BlockSpec((49, 8, LANES), lambda h: (0, h, 0)) for _ in range(8)],
        out_shape=[pltpu.HBM((49, 16, LANES), F32) for _ in range(8)],
        compiler_params=params(FULL, 1),
        name="pack",
    )(me, flat)


def transform(me, block_of, w_ref, xb):
    for s in range(8):
        at = pl.multiple_of(origin(me, s) * 16, 16)
        for b in range(7):
            block = block_of(s, b)
            hi = block.astype(BF16)
            lo = (block - hi.astype(F32)).astype(BF16)
            lanes = pl.ds(b * 128, 128)
            xb[pl.ds(at, 16), lanes] = hi
            xb[pl.ds(at + 128, 16), lanes] = lo
            xb[pl.ds(at + 256, 16), lanes] = hi
    return jnp.dot(w_ref[...], xb[...], preferred_element_type=F32)


def row_copies(sources, a, slots, sems):
    slot = a % 2
    return [
        pltpu.make_async_copy(ref.at[pl.ds(7 * a, 7)], slots.at[slot, i], sems.at[slot, i])
        for i, ref in enumerate(sources)
    ]


def stream_rows(sources, slots, sems, work):
    for copy in row_copies(sources, 0, slots, sems):
        copy.start()

    def step(a, carry):
        @pl.when(a < 6)
        def _():
            for copy in row_copies(sources, a + 1, slots, sems):
                copy.start()

        for copy in row_copies(sources, a, slots, sems):
            copy.wait()
        work(a)
        return carry

    lax.fori_loop(0, 7, step, 0)


BLOCK = [pl.ds(b * 128, 128) for b in range(7)]


def q_rows(t, offset=0):
    return pl.ds(pl.multiple_of(t * 8 + offset, 8), 8)


def early_kernel(*refs):
    me_ref, sources = refs[0], refs[1:17]
    met_ref, w_ref = refs[17:19]
    u, v, zu, zv, adv0, adv1, xb, slots, sems = refs[19:]
    me = me_ref[0]
    sx = met_ref[0]
    sy = met_ref[1]

    def node_row(a):
        for x, (field, slope) in enumerate(((u, zu), (v, zv))):
            both = transform(me, lambda s, b: slots[a % 2, 8 * x + s, b], w_ref, xb)
            field[a] = both[0:128]
            slope[a] = both[128:256]

        def along_b(t, carry):
            q = q_rows(t)
            first = [u[a, q, s] for s in BLOCK]
            second = [v[a, q, s] for s in BLOCK]
            scaled = [item * sy for item in second]
            for field, out in ((first, adv0), (second, adv1)):
                slope = derive(field)
                for b in range(7):
                    out[a, q, BLOCK[b]] = scaled[b] * slope[b]
            return carry

        lax.fori_loop(0, 16, along_b, 0)

    stream_rows(sources, slots, sems, node_row)

    def along_a(t, carry):
        q = q_rows(t)
        for s in BLOCK:
            first = [u[k, q, s] for k in range(7)]
            second = [v[k, q, s] for k in range(7)]
            scaled = [item * sx for item in first]
            for field, out in ((first, adv0), (second, adv1)):
                slope = derive(field)
                for k in range(7):
                    out[k, q, s] = out[k, q, s] + scaled[k] * slope[k]
        return carry

    lax.fori_loop(0, 16, along_a, 0)


def late_kernel(*refs):
    me_ref, sources = refs[0], refs[1:9]
    u, v, zu, zv, adv0, adv1 = refs[9:15]
    met_ref, w_ref, f_ref = refs[15:18]
    outs = refs[18:26]
    xb, w, zw, sum0, div, forward, db = refs[26:]
    me = me_ref[0]
    sx = met_ref[0]
    sy = met_ref[1]
    for s in range(8):
        at = pl.ds(pl.multiple_of(target(me, s) * 16, 16), 16)
        forward[s * 16 : s * 16 + 16] = f_ref[at]

    def node_row(a, carry):
        both = transform(me, lambda s, b: sources[s][7 * a + b], w_ref, xb)
        w[a] = both[0:128]
        zw[...] = both[128:256]

        def along_b(t, carry):
            q = q_rows(t)
            q2 = q_rows(t, 128)
            third = [w[a, q, s] for s in BLOCK]
            slope = derive(third)
            line = []
            for b, s in enumerate(BLOCK):
                sum0[a, q, s] = adv0[a, q, s] + third[b] * zu[a, q, s]
                line.append(adv1[a, q, s] + third[b] * zv[a, q, s])
                div[a, q2, s] = (v[a, q, s] * sy) * slope[b] + third[b] * zw[q, s]
            slope = derive(line)
            for b, s in enumerate(BLOCK):
                div[a, q, s] = sy * slope[b]
            return carry

        lax.fori_loop(0, 16, along_b, 0)
        return carry

    lax.fori_loop(0, 7, node_row, 0)

    def along_a(t, carry):
        q = q_rows(t)
        q2 = q_rows(t, 128)
        for s in BLOCK:
            slope = derive([w[k, q, s] for k in range(7)])
            for k in range(7):
                div[k, q2, s] = div[k, q2, s] + (u[k, q, s] * sx) * slope[k]
            slope = derive([sum0[k, q, s] for k in range(7)])
            for k in range(7):
                div[k, q, s] = div[k, q, s] + sx * slope[k]
        return carry

    lax.fori_loop(0, 16, along_a, 0)
    area = -1.0 / (sx * sy)
    for k in range(7):
        block = div[k]
        hi = block.astype(BF16)
        db[0:256] = hi
        db[256:512] = (block - hi.astype(F32)).astype(BF16)
        db[512:768] = hi
        spec = jnp.dot(forward[...], db[...], preferred_element_type=F32)
        for b in range(7):
            scale = area * np.float32(WEIGHTS[k] * WEIGHTS[b])
            for s in range(8):
                outs[s][7 * k + b] = spec[s * 16 : s * 16 + 16, b * 128 : b * 128 + 128] * scale


def split_bf16(table):
    table = table.astype(np.float32)
    hi = table.astype(ml_dtypes.bfloat16)
    return hi, (table - hi.astype(np.float32)).astype(ml_dtypes.bfloat16)


def rows_of(c, n):
    return pl.ds(pl.multiple_of(c * 392 + n * 8, 8), 8)


def metric_values(met_ref):
    sx, sy = met_ref[0], met_ref[1]
    ratio = sx / sy
    back = sy / sx
    return ratio, back, 1.0 / (sx * sy)


def inverse_divisor(ratio, back, area, wave):
    return 1.0 / (0.5 * (ratio + back) + (wave * MASS_REF) * area)


def store_rims(field, c, east_ref, west_ref):
    for b in range(7):
        east_ref[pl.ds(c * 8 + b, 1), :] = field[42 + b][7:8]
        west_ref[pl.ds(c * 8 + b, 1), :] = field[b][0:1]


def apply_operator(v, wave, ratio, back, area):
    kind = [0, 1, 2, 3, 2, 1, 0]
    sub = lax.broadcasted_iota(jnp.int32, (8, LANES), 0)
    lane = lax.broadcasted_iota(jnp.int32, (8, LANES), 1)
    w = [np.float32(WEIGHTS[k]) for k in range(4)]
    ratio_w = [ratio * w[k] for k in range(4)]
    back_w = [back * w[k] for k in range(4)]
    mass = wave * area
    diag = {}
    for i in range(4):
        for j in range(i, 4):
            rim = PENALTY * ((i == 0) + (j == 0))
            diag[i, j] = mass * np.float32(WEIGHTS[i] * WEIGHTS[j]) + np.float32(rim)
    out = [None] * 49
    for b in range(7):
        column = stiffen([v[7 * a + b] for a in range(7)])
        for a in range(7):
            key = tuple(sorted((kind[a], kind[b])))
            out[7 * a + b] = column[a] * ratio_w[kind[b]] + v[7 * a + b] * diag[key]
    for a in range(7):
        line = stiffen([v[7 * a + b] for b in range(7)])
        for b in range(7):
            out[7 * a + b] = out[7 * a + b] + line[b] * back_w[kind[a]]
    ten = np.float32(PENALTY)
    for b in range(7):
        before = jnp.where(sub == 0, 0.0, pltpu.roll(v[42 + b], 1, 0))
        after = jnp.where(sub == 7, 0.0, pltpu.roll(v[b], 7, 0))
        out[b] = out[b] - ten * before
        out[42 + b] = out[42 + b] - ten * after
    for a in range(7):
        south = jnp.where(lane == 0, 0.0, pltpu.roll(v[7 * a + 6], 1, 1))
        north = jnp.where(lane == 127, 0.0, pltpu.roll(v[7 * a], 127, 1))
        out[7 * a] = out[7 * a] - ten * south
        out[7 * a + 6] = out[7 * a + 6] - ten * north
    return out


def first_kernel(me_ref, wave_ref, *refs):
    recv, (met_ref, r_ref, p_ref, east_ref, west_ref) = refs[:8], refs[8:]
    rows = [origin(me_ref[0], s) for s in range(8)]

    def unpack(n, carry):
        for s in range(8):
            r_ref[pl.ds(n * 8 + rows[s], 16, stride=392), :] = recv[s][n]
        return carry

    lax.fori_loop(0, 49, unpack, 0, unroll=7)
    east_ref[...] = jnp.zeros_like(east_ref)
    west_ref[...] = jnp.zeros_like(west_ref)
    ratio, back, area = metric_values(met_ref)

    def step(c, carry):
        inv = inverse_divisor(ratio, back, area, wave_ref[c])
        field = block_solve([r_ref[rows_of(c, n), :] for n in range(49)])
        field = [item * inv for item in field]
        for n in range(49):
            p_ref[rows_of(c, n), :] = field[n]
        store_rims(field, c, east_ref, west_ref)
        return carry

    lax.fori_loop(0, 16, step, 0)


def rim_fix(value, kind, c, b, edge_ref):
    sub = lax.broadcasted_iota(jnp.int32, (8, LANES), 0)
    row = 0 if kind == "west" else 7
    return jnp.where(sub == row, value - np.float32(PENALTY) * edge_ref[pl.ds(c * 8 + b, 1), :], value)


def local_image_kernel(wave_ref, p_ref, met_ref, q_ref):
    ratio, back, area = metric_values(met_ref)

    def image(c, carry):
        v = [p_ref[rows_of(c, n), :] for n in range(49)]
        out = apply_operator(v, wave_ref[c], ratio, back, area)
        for n in range(49):
            q_ref[rows_of(c, n), :] = out[n]
        return carry

    lax.fori_loop(0, 16, image, 0)


def second_kernel(
    wave_ref, local_ref, met_ref, west_in, east_in, q_ref, s_ref, east_ref, west_ref
):
    east_ref[...] = jnp.zeros_like(east_ref)
    west_ref[...] = jnp.zeros_like(west_ref)
    ratio, back, area = metric_values(met_ref)

    def search(c, carry):
        inv = inverse_divisor(ratio, back, area, wave_ref[c])
        field = [local_ref[rows_of(c, n), :] for n in range(49)]
        for b in range(7):
            field[b] = rim_fix(field[b], "west", c, b, west_in)
            field[42 + b] = rim_fix(field[42 + b], "east", c, b, east_in)
        for n in range(49):
            q_ref[rows_of(c, n), :] = field[n]
        field = block_solve(field)
        field = [item * inv for item in field]
        for n in range(49):
            s_ref[rows_of(c, n), :] = field[n]
        store_rims(field, c, east_ref, west_ref)
        return carry

    lax.fori_loop(0, 16, search, 0)


def third_kernel(wave_ref, r_ref, q_ref, s_ref, met_ref, t_ref, acc_ref):
    ratio, back, area = metric_values(met_ref)

    def image(c, carry):
        v = [s_ref[rows_of(c, n), :] for n in range(49)]
        out = apply_operator(v, wave_ref[c], ratio, back, area)
        sums = [None] * 5
        for n in range(49):
            t_ref[rows_of(c, n), :] = out[n]
            q, r, t = q_ref[rows_of(c, n), :], r_ref[rows_of(c, n), :], out[n]
            for k, term in enumerate((q * q, r * q, t * q, t * t, r * t)):
                sums[k] = term if sums[k] is None else sums[k] + term
        for k in range(5):
            acc_ref[k, pl.ds(c, 1), :] = jnp.sum(sums[k], axis=0, keepdims=True)
        return carry

    lax.fori_loop(0, 16, image, 0)


def product_kernel(r_ref, q_ref, t_ref, acc_ref, west_in, east_in, dots_ref, add_ref, table_ref, sem):
    def step(c, carry):
        tq = jnp.zeros((1, LANES), F32)
        tt, rt = tq, tq
        for b in range(7):
            for n, row, edge_ref in ((b, 0, west_in), (42 + b, 7, east_in)):
                at = pl.ds(c * 392 + n * 8 + row, 1)
                change = -np.float32(PENALTY) * edge_ref[pl.ds(c * 8 + b, 1), :]
                tq = tq + change * q_ref[at, :]
                rt = rt + change * r_ref[at, :]
                tt = tt + change * (2.0 * t_ref[at, :] + change)
        for k, item in enumerate((tq, tt, rt)):
            add_ref[k, pl.ds(c, 1), :] = item
        return carry

    lax.fori_loop(0, 16, step, 0)
    lane = lax.broadcasted_iota(jnp.int32, (16, LANES), 1)
    table = jnp.zeros((16, LANES), F32)
    for k in range(5):
        total = acc_ref[k] if k < 2 else acc_ref[k] + add_ref[k - 2]
        table = jnp.where(lane == k, jnp.sum(total, axis=1, keepdims=True), table)
    for d in range(16):
        table_ref[d] = table
    copy = pltpu.make_async_copy(table_ref, dots_ref, sem)
    copy.start()
    copy.wait()


def last_kernel(
    dots_ref, r_ref, p_ref, q_ref, s_ref, t_ref, west_in, east_in,
    pres_ref, resid_ref, coef_ref, pres_buf, resid_buf, sems,
):
    total = dots_ref[0]
    for d in range(1, 16):
        total = total + dots_ref[d]
    lane = lax.broadcasted_iota(jnp.int32, (16, LANES), 1)

    def pick(k):
        return jnp.sum(jnp.where(lane == k, total, 0.0), axis=1, keepdims=True)

    qq, rq, tq, tt, rt = [pick(k) for k in range(5)]
    alpha = rq / qq
    gamma = tq / qq
    lam = (rt - gamma * rq) / (tt - gamma * tq)
    coef_ref[0] = jnp.broadcast_to(alpha - lam * gamma, (16, LANES))
    coef_ref[1] = jnp.broadcast_to(lam, (16, LANES))

    def copies(c):
        at = pl.ds(pl.multiple_of(c * 392, 8), 392)
        return (
            pltpu.make_async_copy(pres_buf.at[at, :], pres_ref.at[at, :], sems.at[0, c]),
            pltpu.make_async_copy(resid_buf.at[at, :], resid_ref.at[at, :], sems.at[1, c]),
        )

    def step(c, carry):
        first = coef_ref[0, pl.ds(c, 1), :]
        second = coef_ref[1, pl.ds(c, 1), :]
        for n in range(49):
            at = rows_of(c, n)
            t = t_ref[at, :]
            if n < 7:
                t = rim_fix(t, "west", c, n, west_in)
            if n >= 42:
                t = rim_fix(t, "east", c, n - 42, east_in)
            pres_buf[at, :] = first * p_ref[at, :] + second * s_ref[at, :]
            resid_buf[at, :] = r_ref[at, :] - first * q_ref[at, :] - second * t
        for copy in copies(c):
            copy.start()
        return carry

    lax.fori_loop(0, 16, step, 0)

    def finish(c, carry):
        for copy in copies(c):
            copy.wait()
        return carry

    lax.fori_loop(0, 16, finish, 0)


FIELD = (16 * 392, LANES)
RIM = (16 * 8, LANES)


def call(kernel, name, inputs, outs, limit, scratch=(), smem=(), any_in=(), hbm=(), cost=None):
    specs = [
        pl.BlockSpec(
            memory_space=pltpu.SMEM if i in smem else pl.ANY if i in any_in else pltpu.VMEM
        )
        for i in range(len(inputs))
    ]
    out_specs = [
        pl.BlockSpec(memory_space=pltpu.HBM if i in hbm else pltpu.VMEM) for i in range(len(outs))
    ]
    return pl.pallas_call(
        kernel,
        in_specs=specs,
        out_specs=out_specs,
        out_shape=[jax.ShapeDtypeStruct(s, F32) for s in outs],
        scratch_shapes=list(scratch),
        compiler_params=params(limit),
        cost_estimate=cost and pl.CostEstimate(flops=0, bytes_accessed=cost, transcendentals=0),
        name=name,
    )(*inputs)


def body(velocity, metric):
    modes_here = velocity.shape[1]
    basis, forward, modal_diff, wave_all = mode_tables(modes_here * lax.axis_size("fourier"))
    mine = lax.axis_index("fourier")
    me = mine.astype(jnp.int32).reshape(1)
    wave = lax.dynamic_slice_in_dim(jnp.asarray(wave_all, F32), mine * modes_here, modes_here)
    met_row = lax.dynamic_slice_in_dim(metric, mine, 1, 1)
    hi, lo = split_bf16(np.concatenate([basis, basis @ modal_diff], axis=0))
    to_planes = jnp.asarray(np.concatenate([hi, hi, lo], axis=1))
    hi, lo = split_bf16(np.concatenate([forward, modal_diff @ forward], axis=1))
    to_modes = jnp.asarray(np.concatenate([hi, hi, lo], axis=1))

    flat = pltpu.with_memory_space_constraint(velocity.reshape(3 * 16 * 392, LANES), pltpu.HBM)
    gathered = []
    for x in range(3):
        packed = pack(me, flat, x)
        blocks = [packed[0]] + [permute(packed[s], s) for s in range(1, 8)]
        if x < 2:
            blocks = [pltpu.with_memory_space_constraint(item, pltpu.HBM) for item in blocks]
        gathered.append(blocks)

    plane_field = (7, 128, 896)
    early = call(
        early_kernel,
        "early",
        (me, *gathered[0], *gathered[1], met_row, to_planes),
        [plane_field] * 6,
        8,
        [
            pltpu.VMEM((384, 896), BF16),
            pltpu.VMEM((2, 16, 7, 16, LANES), F32),
            pltpu.SemaphoreType.DMA((2, 16)),
        ],
        smem=(0,),
        any_in=range(1, 17),
        cost=40 * MIB,
    )
    source = call(
        late_kernel,
        "late",
        (me, *gathered[2], *early, met_row, to_planes, to_modes),
        [(49, 16, LANES)] * 8,
        22,
        [
            pltpu.VMEM((384, 896), BF16),
            pltpu.VMEM(plane_field, F32),
            pltpu.VMEM((128, 896), F32),
            pltpu.VMEM(plane_field, F32),
            pltpu.VMEM((7, 256, 896), F32),
            pltpu.VMEM((128, 768), BF16),
            pltpu.VMEM((768, 896), BF16),
        ],
        smem=(0,),
        cost=40 * MIB,
    )
    recv = [source[0]] + [permute(source[s], s) for s in range(1, 8)]

    size = lax.axis_size("plane")
    up = [(i, i + 1) for i in range(size - 1)]
    down = [(j, i) for i, j in up]

    def exchange(east, west):
        return lax.ppermute(east, "plane", up), lax.ppermute(west, "plane", down)

    r, p1, east, west = call(
        first_kernel,
        "first",
        (me, wave, *recv, metric),
        [FIELD, FIELD, RIM, RIM],
        24,
        smem=(0, 1),
    )
    west_in, east_in = exchange(east, west)
    (local,) = call(
        local_image_kernel, "local_image", (wave, p1, metric), [FIELD], 16, smem=(0,), cost=8 * MIB
    )
    q1, s, east, west = call(
        second_kernel,
        "second",
        (wave, local, metric, west_in, east_in),
        [FIELD, FIELD, RIM, RIM],
        16,
        smem=(0,),
    )
    west_in, east_in = exchange(east, west)
    t, acc = call(
        third_kernel,
        "third",
        (wave, r, q1, s, metric),
        [FIELD, (5, 16, LANES)],
        16,
        smem=(0,),
        cost=12 * MIB,
    )
    (dots,) = call(
        product_kernel,
        "products",
        (r, q1, t, acc, west_in, east_in),
        [(16, 16, LANES)],
        16,
        [
            pltpu.VMEM((3, 16, LANES), F32),
            pltpu.VMEM((16, 16, LANES), F32),
            pltpu.SemaphoreType.DMA,
        ],
        hbm=(0,),
    )
    dots = lax.all_to_all(dots, "plane", 0, 0, tiled=True)
    pressure, residual = call(
        last_kernel,
        "last",
        (dots, r, p1, q1, s, t, west_in, east_in),
        [FIELD, FIELD],
        24,
        [
            pltpu.VMEM((2, 16, LANES), F32),
            pltpu.VMEM(FIELD, F32),
            pltpu.VMEM(FIELD, F32),
            pltpu.SemaphoreType.DMA((2, 16)),
        ],
        hbm=(0, 1),
    )
    shape = velocity.shape[1:]
    return pressure.reshape(shape), residual.reshape(shape)


def solution(mesh):
    in_specs = (P(None, "fourier", None, "plane", None), P(None, "plane", None))
    out_specs = (P("fourier", None, "plane", None), P("fourier", None, "plane", None))
    return jax.shard_map(body, mesh=mesh, in_specs=in_specs, out_specs=out_specs, check_vma=False)
```

```python
import jax
import jax.numpy as jnp
import ml_dtypes
import numpy as np
from jax import lax
from jax.experimental import pallas as pl
from jax.experimental.pallas import tpu as pltpu
from jax.sharding import PartitionSpec as P

PENALTY = 10.0
BETA = 0.5
MASS_REF = 0.08
LANES = 128
F32 = jnp.float32
BF16 = jnp.bfloat16
MIB = 1 << 20
FULL = 60


def node_tables():
    nodes = np.array(
        [
            -1.0,
            -0.830223896278567,
            -0.4688487934707142,
            0.0,
            0.4688487934707142,
            0.830223896278567,
            1.0,
        ]
    )
    weights = np.array(
        [
            1.0 / 21.0,
            0.2768260473615659,
            0.4317453812098627,
            0.4876190476190476,
            0.4317453812098627,
            0.2768260473615659,
            1.0 / 21.0,
        ]
    )
    identity = np.eye(7)
    differ = nodes[:, None] - nodes[None, :] + identity
    bary = 1.0 / np.prod(differ, axis=1)
    off_diag = np.where(identity > 0.5, 0.0, bary[None, :] / bary[:, None] / differ)
    deriv = off_diag - identity * off_diag.sum(axis=1)[:, None]
    weight_diag = identity * weights[None, :]
    stiff = deriv.T @ weight_diag @ deriv
    side = np.where((np.arange(7) == 0) | (np.arange(7) == 6), 1.0, 0.0)
    rim = (side[:, None] + side[None, :]).reshape(49)
    system = np.kron(stiff, weight_diag) + np.kron(weight_diag, stiff)
    system = system + PENALTY * np.eye(49) * rim[None, :]
    system = system.astype(np.float32).astype(np.float64)
    return weights, deriv, stiff, np.linalg.inv(system)


def mode_tables(length):
    index = np.arange(length)
    wavenum = index // 2
    wavenum[1] = length // 2
    angles = 2.0 * np.pi * np.outer(index, wavenum) / length
    use_cos = (index % 2 == 0) | (index == 1)
    basis = np.where(use_cos[None, :], np.cos(angles), np.sin(angles))
    factor = np.full(length, 2.0 / length)
    factor[:2] = 1.0 / length
    forward = factor[:, None] * basis.T
    modal_diff = np.zeros((length, length))
    even = np.arange(2, length, 2)
    modal_diff[even, even + 1] = BETA * wavenum[even]
    modal_diff[even + 1, even] = -BETA * wavenum[even]
    wave_sq = (BETA * wavenum) ** 2
    return basis, forward, modal_diff, wave_sq


WEIGHTS, DERIV, STIFF, BLOCK_INV = node_tables()

ANALYSIS = np.zeros((7, 7))
SYNTHESIS = np.zeros((7, 7))
for _k in range(3):
    ANALYSIS[_k, _k] = ANALYSIS[_k, 6 - _k] = 1.0
    ANALYSIS[4 + _k, _k] = 1.0
    ANALYSIS[4 + _k, 6 - _k] = -1.0
    SYNTHESIS[_k, _k] = SYNTHESIS[6 - _k, _k] = 1.0
    SYNTHESIS[_k, 4 + _k] = 1.0
    SYNTHESIS[6 - _k, 4 + _k] = -1.0
ANALYSIS[3, 3] = SYNTHESIS[3, 3] = 1.0


def parity_form(matrix):
    return np.linalg.inv(SYNTHESIS) @ matrix @ np.linalg.inv(ANALYSIS)


DERIV_P = parity_form(DERIV)
STIFF_P = parity_form(STIFF)
_S2 = np.kron(ANALYSIS, ANALYSIS)
_R2 = np.kron(SYNTHESIS, SYNTHESIS)
BLOCK_P = np.linalg.inv(_R2) @ BLOCK_INV @ np.linalg.inv(_S2)
BLOCK_P = BLOCK_P.reshape(7, 7, 7, 7)


def analyse(v):
    return [v[0] + v[6], v[1] + v[5], v[2] + v[4], v[3], v[0] - v[6], v[1] - v[5], v[2] - v[4]]


def synthesise(g):
    return [
        g[0] + g[4],
        g[1] + g[5],
        g[2] + g[6],
        g[3],
        g[2] - g[6],
        g[1] - g[5],
        g[0] - g[4],
    ]


def mat_rows(matrix, v):
    out = []
    for row in matrix:
        acc = None
        for coef, item in zip(row, v):
            if abs(coef) > 1e-11:
                term = item * np.float32(coef)
                acc = term if acc is None else acc + term
        out.append(acc)
    return out


def derive(v):
    g = analyse(v)
    even = mat_rows(DERIV_P[:4, 4:], g[4:])
    odd = mat_rows(DERIV_P[4:, :4], g[:4])
    out = [even[k] + odd[k] for k in range(3)]
    return out + [even[3]] + [even[k] - odd[k] for k in (2, 1, 0)]


def stiffen(v):
    g = analyse(v)
    return synthesise(mat_rows(STIFF_P[:4, :4], g[:4]) + mat_rows(STIFF_P[4:, 4:], g[4:]))


def symmetric_sector(table, x, size):
    pairs = [(i, j) for i in range(size) for j in range(i, size)]
    anti = [(i, j) for i in range(size) for j in range(i + 1, size)]
    plus = [x[i][j] if i == j else x[i][j] + x[j][i] for i, j in pairs]
    minus = [x[i][j] - x[j][i] for i, j in anti]

    def sym_row(i, j):
        return [0.5 * (table[i, j, k, l] + table[i, j, l, k]) for k, l in pairs]

    def anti_row(i, j):
        return [0.5 * (table[i, j, k, l] - table[i, j, l, k]) for k, l in anti]

    top = dict(zip(pairs, mat_rows([sym_row(i, j) for i, j in pairs], plus)))
    low = dict(zip(anti, mat_rows([anti_row(i, j) for i, j in anti], minus)))
    out = [[None] * size for _ in range(size)]
    for i, j in pairs:
        if i == j:
            out[i][j] = top[i, j]
        else:
            out[i][j] = top[i, j] + low[i, j]
            out[j][i] = top[i, j] - low[i, j]
    return out


def block_solve(v):
    part = [[None] * 7 for _ in range(7)]
    for b in range(7):
        column = analyse([v[7 * a + b] for a in range(7)])
        for k in range(7):
            part[k][b] = column[k]
    part = [analyse(part[k]) for k in range(7)]
    out = [[None] * 7 for _ in range(7)]
    ev, od = slice(0, 4), slice(4, 7)
    for rows, cols in ((ev, ev), (od, od), (ev, od), (od, ev)):
        ri, ci = range(7)[rows], range(7)[cols]
        x = [[part[i][j] for j in ci] for i in ri]
        table = BLOCK_P[rows, cols, rows, cols]
        if rows == cols:
            y = symmetric_sector(table, x, len(ri))
        else:
            n = len(ri) * len(ci)
            flat = mat_rows(table.reshape(n, n), [x[i][j] for i in range(len(ri)) for j in range(len(ci))])
            y = [flat[i * len(ci) : (i + 1) * len(ci)] for i in range(len(ri))]
        for i, row in zip(ri, y):
            for j, item in zip(ci, row):
                out[i][j] = item
    out = [synthesise(out[k]) for k in range(7)]
    res = [None] * 49
    for b in range(7):
        column = synthesise([out[k][b] for k in range(7)])
        for a in range(7):
            res[7 * a + b] = column[a]
    return res


def params(limit_mib, grid=None):
    semantics = None if grid is None else ("arbitrary",) * grid
    return pltpu.CompilerParams(vmem_limit_bytes=limit_mib * MIB, dimension_semantics=semantics)


STEPS = ((0, 0), (1, 0), (3, 0), (2, 0), (1, 1), (3, 1), (2, 1), (0, 1))


PAIRS = tuple((STEPS.index((d, 0)), STEPS.index((d, 1))) for d in range(4))


def partner(me, d, flip):
    core = me % 2
    return ((me // 2 + d) % 4) * 2 + (core + flip - 2 * core * flip)


def permute(value, step):
    d, flip = STEPS[step]
    return lax.ppermute(value, "fourier", [(i, partner(i, d, flip)) for i in range(8)])


def target(me, step):
    return partner(me, *STEPS[step])


def origin(me, step):
    d, flip = STEPS[step]
    return partner(me, (4 - d) % 4, flip)


def pack_kernel(me_ref, block_ref, *out_refs):
    me = me_ref[0]
    in_ref = block_ref.reshape(8 * 392, LANES)
    rows = [target(me, s) for s in range(8)]

    def step(n, carry):
        for s in range(8):
            out_refs[s][0, n] = in_ref[pl.ds(n * 8 + rows[s], 8, stride=392), :]
        return carry

    lax.fori_loop(0, 49, step, 0, unroll=7)


def pack(me, split, x):
    return pl.pallas_call(
        pack_kernel,
        grid=(2,),
        in_specs=[
            pl.BlockSpec(memory_space=pltpu.SMEM),
            pl.BlockSpec((1, 4, 1, 2, 392, LANES), lambda p: (x, 0, p, 0, 0, 0)),
        ],
        out_specs=[pl.BlockSpec((1, 49, 8, LANES), lambda p: (p, 0, 0, 0)) for _ in range(8)],
        out_shape=[pltpu.HBM((2, 49, 8, LANES), F32) for _ in range(8)],
        compiler_params=params(FULL, 1),
        name="pack",
    )(me, split)


def transform(me, block_of, w_ref, xb, field, slope):
    core = me % 2
    for first, second in PAIRS:
        at = pl.multiple_of((origin(me, first) // 2) * 16, 16)
        for b in range(7):
            lanes = pl.ds(b * 128, 128)
            for p in range(2):
                block = jnp.concatenate([block_of(first, p, b), block_of(second, p, b)], axis=0)
                hi = block.astype(BF16)
                xb[pl.ds(at + 192 * p, 16), lanes] = hi
                xb[pl.ds(at + 192 * p + 64, 16), lanes] = (block - hi.astype(F32)).astype(BF16)
                xb[pl.ds(at + 192 * p + 128, 16), lanes] = hi
    even = jnp.dot(w_ref[core, 0], xb[0:192], preferred_element_type=F32)
    odd = jnp.dot(w_ref[core, 1], xb[192:384], preferred_element_type=F32)
    field[0:64] = even[0:64] + odd[0:64]
    field[64:128] = even[0:64] - odd[0:64]
    slope[0:64] = even[64:128] + odd[64:128]
    slope[64:128] = even[64:128] - odd[64:128]


def row_copies(sources, a, slots, sems):
    slot = a % 2
    return [
        pltpu.make_async_copy(ref.at[:, pl.ds(7 * a, 7)], slots.at[slot, i], sems.at[slot, i])
        for i, ref in enumerate(sources)
    ]


def stream_rows(sources, slots, sems, work):
    for copy in row_copies(sources, 0, slots, sems):
        copy.start()

    def step(a, carry):
        @pl.when(a < 6)
        def _():
            for copy in row_copies(sources, a + 1, slots, sems):
                copy.start()

        for copy in row_copies(sources, a, slots, sems):
            copy.wait()
        work(a)
        return carry

    lax.fori_loop(0, 7, step, 0)


BLOCK = [pl.ds(b * 128, 128) for b in range(7)]


def q_rows(t, offset=0):
    return pl.ds(pl.multiple_of(t * 8 + offset, 8), 8)


def early_kernel(*refs):
    me_ref, sources = refs[0], refs[1:17]
    met_ref, w_ref = refs[17:19]
    u, v, zu, zv, adv0, adv1, xb, slots, sems = refs[19:]
    me = me_ref[0]
    sx = met_ref[0]
    sy = met_ref[1]

    def node_row(a):
        for x, (field, slope) in enumerate(((u, zu), (v, zv))):
            transform(
                me, lambda s, p, b: slots[a % 2, 8 * x + s, p, b], w_ref, xb, field.at[a], slope.at[a]
            )

        def along_b(t, carry):
            q = q_rows(t)
            first = [u[a, q, s] for s in BLOCK]
            second = [v[a, q, s] for s in BLOCK]
            scaled = [item * sy for item in second]
            for field, out, scale in ((first, adv0, sx), (second, adv1, sy)):
                slope = derive(field)
                for b in range(7):
                    out[a, q, BLOCK[b]] = (scaled[b] * slope[b]) * scale
            for s in BLOCK:
                zu[a, q, s] = zu[a, q, s] * sx
                zv[a, q, s] = zv[a, q, s] * sy
            return carry

        lax.fori_loop(0, 16, along_b, 0)

    stream_rows(sources, slots, sems, node_row)

    def along_a(t, carry):
        q = q_rows(t)
        for s in BLOCK:
            first = [u[k, q, s] for k in range(7)]
            second = [v[k, q, s] for k in range(7)]
            scaled = [item * sx for item in first]
            for field, out, scale in ((first, adv0, sx), (second, adv1, sy)):
                slope = derive(field)
                for k in range(7):
                    out[k, q, s] = out[k, q, s] + (scaled[k] * slope[k]) * scale
            for k in range(7):
                u[k, q, s] = scaled[k]
                v[k, q, s] = second[k] * sy
        return carry

    lax.fori_loop(0, 16, along_a, 0)


def late_kernel(*refs):
    me_ref, sources = refs[0], refs[1:9]
    u, v, zu, zv, adv0, adv1 = refs[9:15]
    met_ref, w_ref, f_ref = refs[15:18]
    outs = refs[18:26]
    xb, w, zw, sum0, div, forward, db = refs[26:]
    me = me_ref[0]
    sx = met_ref[0]
    sy = met_ref[1]
    for d, (first, _) in enumerate(PAIRS):
        at = pl.ds(pl.multiple_of((target(me, first) // 2) * 16, 16), 16)
        for p in range(2):
            forward[p, d * 16 : d * 16 + 16] = f_ref[me % 2, p, 0, at]
            forward[p, 64 + d * 16 : 80 + d * 16] = f_ref[me % 2, p, 1, at]

    def node_row(a, carry):
        transform(me, lambda s, p, b: sources[s][p, 7 * a + b], w_ref, xb, w.at[a], zw)

        def along_b(t, carry):
            q = q_rows(t)
            q2 = q_rows(t, 128)
            third = [w[a, q, s] for s in BLOCK]
            slope = derive(third)
            line = []
            for b, s in enumerate(BLOCK):
                sum0[a, q, s] = adv0[a, q, s] + third[b] * zu[a, q, s]
                line.append(adv1[a, q, s] + third[b] * zv[a, q, s])
                div[a, q2, s] = v[a, q, s] * slope[b] + third[b] * zw[q, s]
            slope = derive(line)
            for b, s in enumerate(BLOCK):
                div[a, q, s] = slope[b]
            return carry

        lax.fori_loop(0, 16, along_b, 0, unroll=4)
        return carry

    lax.fori_loop(0, 7, node_row, 0)

    def along_a(t, carry):
        q = q_rows(t)
        q2 = q_rows(t, 128)
        for s in BLOCK:
            slope = derive([w[k, q, s] for k in range(7)])
            for k in range(7):
                div[k, q2, s] = div[k, q2, s] + u[k, q, s] * slope[k]
            slope = derive([sum0[k, q, s] for k in range(7)])
            for k in range(7):
                div[k, q, s] = div[k, q, s] + slope[k]
        return carry

    lax.fori_loop(0, 16, along_a, 0, unroll=2)
    area = -1.0 / (sx * sy)
    for k in range(7):
        for p in range(2):
            for i in range(2):
                one, two = div[k, 128 * i : 128 * i + 64], div[k, 128 * i + 64 : 128 * i + 128]
                block = one + two if p == 0 else one - two
                hi = block.astype(BF16)
                db[k % 2, p, 64 * i : 64 * i + 64] = hi
                db[k % 2, p, 128 + 64 * i : 192 + 64 * i] = (block - hi.astype(F32)).astype(BF16)
        for p in range(2):
            both = jnp.dot(forward[p], db[k % 2, p], preferred_element_type=F32)
            spec = both[0:64] + both[64:128]
            for b in range(7):
                scale = area * np.float32(WEIGHTS[k] * WEIGHTS[b])
                for d, pair in enumerate(PAIRS):
                    for flip, s in enumerate(pair):
                        low = 16 * d + 8 * flip
                        value = spec[low : low + 8, b * 128 : b * 128 + 128] * scale
                        outs[s][7 * k + b, 8 * p : 8 * p + 8] = value


def parity_columns(core, parity):
    return [
        16 * (2 * y + (core + flip) % 2) + 4 * g + 2 * parity + r
        for y in range(4)
        for flip in range(2)
        for g in range(4)
        for r in range(2)
    ]


def wave_tables(basis, forward, modal_diff):
    planes, modes = [], []
    for core in range(2):
        for parity in range(2):
            c = parity_columns(core, parity)
            hi, lo = split_bf16(np.concatenate([basis[:64, c], (basis @ modal_diff)[:64, c]]))
            planes.append(np.concatenate([hi, hi, lo], axis=1))
            back = np.concatenate([forward[c, :64], (modal_diff @ forward)[c, :64]], axis=1)
            hi, lo = split_bf16(back)
            modes.append(np.stack([np.concatenate([hi, hi], 1), np.concatenate([lo, 0 * lo], 1)]))
    return (
        jnp.asarray(np.stack(planes).reshape(2, 2, 128, 192)),
        jnp.asarray(np.stack(modes).reshape(2, 2, 2, 64, 256)),
    )


def split_bf16(table):
    table = table.astype(np.float32)
    hi = table.astype(ml_dtypes.bfloat16)
    return hi, (table - hi.astype(np.float32)).astype(ml_dtypes.bfloat16)


def rows_of(c, n):
    return pl.ds(pl.multiple_of(c * 392 + n * 8, 8), 8)


def metric_values(met_ref):
    sx, sy = met_ref[0], met_ref[1]
    ratio = sx / sy
    back = sy / sx
    return ratio, back, 1.0 / (sx * sy)


def inverse_divisor(ratio, back, area, wave):
    return 1.0 / (0.5 * (ratio + back) + (wave * MASS_REF) * area)


def store_rims(field, c, east_ref, west_ref):
    for b in range(7):
        east_ref[pl.ds(c * 8 + b, 1), :] = field[42 + b][7:8]
        west_ref[pl.ds(c * 8 + b, 1), :] = field[b][0:1]


def apply_operator(v, wave, ratio, back, area):
    kind = [0, 1, 2, 3, 2, 1, 0]
    sub = lax.broadcasted_iota(jnp.int32, (8, LANES), 0)
    lane = lax.broadcasted_iota(jnp.int32, (8, LANES), 1)
    w = [np.float32(WEIGHTS[k]) for k in range(4)]
    ratio_w = [ratio * w[k] for k in range(4)]
    back_w = [back * w[k] for k in range(4)]
    mass = wave * area
    diag = {}
    for i in range(4):
        for j in range(i, 4):
            rim = PENALTY * ((i == 0) + (j == 0))
            diag[i, j] = mass * np.float32(WEIGHTS[i] * WEIGHTS[j]) + np.float32(rim)
    out = [None] * 49
    for b in range(7):
        column = stiffen([v[7 * a + b] for a in range(7)])
        for a in range(7):
            key = tuple(sorted((kind[a], kind[b])))
            out[7 * a + b] = column[a] * ratio_w[kind[b]] + v[7 * a + b] * diag[key]
    for a in range(7):
        line = stiffen([v[7 * a + b] for b in range(7)])
        for b in range(7):
            out[7 * a + b] = out[7 * a + b] + line[b] * back_w[kind[a]]
    ten = np.float32(PENALTY)
    for b in range(7):
        before = jnp.where(sub == 0, 0.0, pltpu.roll(v[42 + b], 1, 0))
        after = jnp.where(sub == 7, 0.0, pltpu.roll(v[b], 7, 0))
        out[b] = out[b] - ten * before
        out[42 + b] = out[42 + b] - ten * after
    for a in range(7):
        south = jnp.where(lane == 0, 0.0, pltpu.roll(v[7 * a + 6], 1, 1))
        north = jnp.where(lane == 127, 0.0, pltpu.roll(v[7 * a], 127, 1))
        out[7 * a] = out[7 * a] - ten * south
        out[7 * a + 6] = out[7 * a + 6] - ten * north
    return out


def first_kernel(me_ref, wave_ref, *refs):
    recv, (met_ref, r_ref, p_ref, east_ref, west_ref) = refs[:8], refs[8:]
    rows = [origin(me_ref[0], s) for s in range(8)]

    def unpack(n, carry):
        for s in range(8):
            r_ref[pl.ds(n * 8 + rows[s], 16, stride=392), :] = recv[s][n]
        return carry

    lax.fori_loop(0, 49, unpack, 0, unroll=7)
    east_ref[...] = jnp.zeros_like(east_ref)
    west_ref[...] = jnp.zeros_like(west_ref)
    ratio, back, area = metric_values(met_ref)

    def step(c, carry):
        inv = inverse_divisor(ratio, back, area, wave_ref[c])
        field = block_solve([r_ref[rows_of(c, n), :] for n in range(49)])
        field = [item * inv for item in field]
        for n in range(49):
            p_ref[rows_of(c, n), :] = field[n]
        store_rims(field, c, east_ref, west_ref)
        return carry

    lax.fori_loop(0, 16, step, 0)


def rim_fix(value, kind, c, b, edge_ref):
    sub = lax.broadcasted_iota(jnp.int32, (8, LANES), 0)
    row = 0 if kind == "west" else 7
    return jnp.where(sub == row, value - np.float32(PENALTY) * edge_ref[pl.ds(c * 8 + b, 1), :], value)


def local_image_kernel(wave_ref, p_ref, met_ref, q_ref):
    ratio, back, area = metric_values(met_ref)

    def image(c, carry):
        v = [p_ref[rows_of(c, n), :] for n in range(49)]
        out = apply_operator(v, wave_ref[c], ratio, back, area)
        for n in range(49):
            q_ref[rows_of(c, n), :] = out[n]
        return carry

    lax.fori_loop(0, 16, image, 0)


def second_kernel(
    wave_ref, local_ref, met_ref, west_in, east_in, q_ref, s_ref, east_ref, west_ref
):
    east_ref[...] = jnp.zeros_like(east_ref)
    west_ref[...] = jnp.zeros_like(west_ref)
    ratio, back, area = metric_values(met_ref)

    def search(c, carry):
        inv = inverse_divisor(ratio, back, area, wave_ref[c])
        field = [local_ref[rows_of(c, n), :] for n in range(49)]
        for b in range(7):
            field[b] = rim_fix(field[b], "west", c, b, west_in)
            field[42 + b] = rim_fix(field[42 + b], "east", c, b, east_in)
        for n in range(49):
            q_ref[rows_of(c, n), :] = field[n]
        field = block_solve(field)
        field = [item * inv for item in field]
        for n in range(49):
            s_ref[rows_of(c, n), :] = field[n]
        store_rims(field, c, east_ref, west_ref)
        return carry

    lax.fori_loop(0, 16, search, 0)


def third_kernel(wave_ref, r_ref, q_ref, s_ref, met_ref, t_ref, acc_ref):
    ratio, back, area = metric_values(met_ref)

    def image(c, carry):
        v = [s_ref[rows_of(c, n), :] for n in range(49)]
        out = apply_operator(v, wave_ref[c], ratio, back, area)
        sums = [None] * 5
        for n in range(49):
            t_ref[rows_of(c, n), :] = out[n]
            q, r, t = q_ref[rows_of(c, n), :], r_ref[rows_of(c, n), :], out[n]
            for k, term in enumerate((q * q, r * q, t * q, t * t, r * t)):
                sums[k] = term if sums[k] is None else sums[k] + term
        for k in range(5):
            acc_ref[k, pl.ds(c, 1), :] = jnp.sum(sums[k], axis=0, keepdims=True)
        return carry

    lax.fori_loop(0, 16, image, 0)


def product_kernel(r_ref, q_ref, t_ref, acc_ref, west_in, east_in, dots_ref, add_ref, table_ref, sem):
    def step(c, carry):
        tq = jnp.zeros((1, LANES), F32)
        tt, rt = tq, tq
        for b in range(7):
            for n, row, edge_ref in ((b, 0, west_in), (42 + b, 7, east_in)):
                at = pl.ds(c * 392 + n * 8 + row, 1)
                change = -np.float32(PENALTY) * edge_ref[pl.ds(c * 8 + b, 1), :]
                tq = tq + change * q_ref[at, :]
                rt = rt + change * r_ref[at, :]
                tt = tt + change * (2.0 * t_ref[at, :] + change)
        for k, item in enumerate((tq, tt, rt)):
            add_ref[k, pl.ds(c, 1), :] = item
        return carry

    lax.fori_loop(0, 16, step, 0)
    lane = lax.broadcasted_iota(jnp.int32, (16, LANES), 1)
    table = jnp.zeros((16, LANES), F32)
    for k in range(5):
        total = acc_ref[k] if k < 2 else acc_ref[k] + add_ref[k - 2]
        table = jnp.where(lane == k, jnp.sum(total, axis=1, keepdims=True), table)
    for d in range(16):
        table_ref[d] = table
    copy = pltpu.make_async_copy(table_ref, dots_ref, sem)
    copy.start()
    copy.wait()


def last_kernel(
    dots_ref, r_ref, p_ref, q_ref, s_ref, t_ref, west_in, east_in,
    pres_ref, resid_ref, coef_ref, pres_buf, resid_buf, sems,
):
    total = dots_ref[0]
    for d in range(1, 16):
        total = total + dots_ref[d]
    lane = lax.broadcasted_iota(jnp.int32, (16, LANES), 1)

    def pick(k):
        return jnp.sum(jnp.where(lane == k, total, 0.0), axis=1, keepdims=True)

    qq, rq, tq, tt, rt = [pick(k) for k in range(5)]
    alpha = rq / qq
    gamma = tq / qq
    lam = (rt - gamma * rq) / (tt - gamma * tq)
    coef_ref[0] = jnp.broadcast_to(alpha - lam * gamma, (16, LANES))
    coef_ref[1] = jnp.broadcast_to(lam, (16, LANES))

    def copies(c):
        mode = 4 * ((c // 2) % 4) + 2 * (c // 8) + c % 2
        at = pl.ds(pl.multiple_of(c * 392, 8), 392)
        to = pl.ds(pl.multiple_of(mode * 392, 8), 392)
        return (
            pltpu.make_async_copy(pres_buf.at[at, :], pres_ref.at[to, :], sems.at[0, c]),
            pltpu.make_async_copy(resid_buf.at[at, :], resid_ref.at[to, :], sems.at[1, c]),
        )

    def step(c, carry):
        first = coef_ref[0, pl.ds(c, 1), :]
        second = coef_ref[1, pl.ds(c, 1), :]
        for n in range(49):
            at = rows_of(c, n)
            t = t_ref[at, :]
            if n < 7:
                t = rim_fix(t, "west", c, n, west_in)
            if n >= 42:
                t = rim_fix(t, "east", c, n - 42, east_in)
            pres_buf[at, :] = first * p_ref[at, :] + second * s_ref[at, :]
            resid_buf[at, :] = r_ref[at, :] - first * q_ref[at, :] - second * t
        for copy in copies(c):
            copy.start()
        return carry

    lax.fori_loop(0, 16, step, 0)

    def finish(c, carry):
        for copy in copies(c):
            copy.wait()
        return carry

    lax.fori_loop(0, 16, finish, 0)


FIELD = (16 * 392, LANES)
RIM = (16 * 8, LANES)


def call(kernel, name, inputs, outs, limit, scratch=(), smem=(), any_in=(), hbm=(), cost=None):
    specs = [
        pl.BlockSpec(
            memory_space=pltpu.SMEM if i in smem else pl.ANY if i in any_in else pltpu.VMEM
        )
        for i in range(len(inputs))
    ]
    out_specs = [
        pl.BlockSpec(memory_space=pltpu.HBM if i in hbm else pltpu.VMEM) for i in range(len(outs))
    ]
    return pl.pallas_call(
        kernel,
        in_specs=specs,
        out_specs=out_specs,
        out_shape=[jax.ShapeDtypeStruct(s, F32) for s in outs],
        scratch_shapes=list(scratch),
        compiler_params=params(limit),
        cost_estimate=cost and pl.CostEstimate(flops=0, bytes_accessed=cost, transcendentals=0),
        name=name,
    )(*inputs)


def body(velocity, metric):
    modes_here = velocity.shape[1]
    basis, forward, modal_diff, wave_all = mode_tables(modes_here * lax.axis_size("fourier"))
    mine = lax.axis_index("fourier")
    me = mine.astype(jnp.int32).reshape(1)
    wave_all = wave_all.reshape(-1, 4, 2, 2).transpose(0, 2, 1, 3).reshape(-1)
    wave = lax.dynamic_slice_in_dim(jnp.asarray(wave_all, F32), mine * modes_here, modes_here)
    met_row = lax.dynamic_slice_in_dim(metric, mine, 1, 1)
    to_planes, to_modes = wave_tables(basis, forward, modal_diff)

    split = pltpu.with_memory_space_constraint(
        velocity.reshape(3, 4, 2, 2, 392, LANES), pltpu.HBM
    )
    gathered = []
    for x in range(3):
        packed = pack(me, split, x)
        blocks = [packed[0]] + [permute(packed[s], s) for s in range(1, 8)]
        if x < 2:
            blocks = [pltpu.with_memory_space_constraint(item, pltpu.HBM) for item in blocks]
        gathered.append(blocks)

    plane_field = (7, 128, 896)
    early = call(
        early_kernel,
        "early",
        (me, *gathered[0], *gathered[1], met_row, to_planes),
        [plane_field] * 6,
        8,
        [
            pltpu.VMEM((384, 896), BF16),
            pltpu.VMEM((2, 16, 2, 7, 8, LANES), F32),
            pltpu.SemaphoreType.DMA((2, 16)),
        ],
        smem=(0,),
        any_in=range(1, 17),
        cost=40 * MIB,
    )
    source = call(
        late_kernel,
        "late",
        (me, *gathered[2], *early, met_row, to_planes, to_modes),
        [(49, 16, LANES)] * 8,
        22,
        [
            pltpu.VMEM((384, 896), BF16),
            pltpu.VMEM(plane_field, F32),
            pltpu.VMEM((128, 896), F32),
            pltpu.VMEM(plane_field, F32),
            pltpu.VMEM((7, 256, 896), F32),
            pltpu.VMEM((2, 128, 256), BF16),
            pltpu.VMEM((2, 2, 256, 896), BF16),
        ],
        smem=(0,),
        cost=40 * MIB,
    )
    recv = [source[0]] + [permute(source[s], s) for s in range(1, 8)]

    size = lax.axis_size("plane")
    up = [(i, i + 1) for i in range(size - 1)]
    down = [(j, i) for i, j in up]

    def exchange(east, west):
        return lax.ppermute(east, "plane", up), lax.ppermute(west, "plane", down)

    r, p1, east, west = call(
        first_kernel,
        "first",
        (me, wave, *recv, metric),
        [FIELD, FIELD, RIM, RIM],
        24,
        smem=(0, 1),
    )
    west_in, east_in = exchange(east, west)
    (local,) = call(
        local_image_kernel, "local_image", (wave, p1, metric), [FIELD], 16, smem=(0,), cost=8 * MIB
    )
    q1, s, east, west = call(
        second_kernel,
        "second",
        (wave, local, metric, west_in, east_in),
        [FIELD, FIELD, RIM, RIM],
        16,
        smem=(0,),
    )
    west_in, east_in = exchange(east, west)
    t, acc = call(
        third_kernel,
        "third",
        (wave, r, q1, s, metric),
        [FIELD, (5, 16, LANES)],
        16,
        smem=(0,),
        cost=12 * MIB,
    )
    (dots,) = call(
        product_kernel,
        "products",
        (r, q1, t, acc, west_in, east_in),
        [(16, 16, LANES)],
        16,
        [
            pltpu.VMEM((3, 16, LANES), F32),
            pltpu.VMEM((16, 16, LANES), F32),
            pltpu.SemaphoreType.DMA,
        ],
        hbm=(0,),
    )
    dots = lax.all_to_all(dots, "plane", 0, 0, tiled=True)
    pressure, residual = call(
        last_kernel,
        "last",
        (dots, r, p1, q1, s, t, west_in, east_in),
        [FIELD, FIELD],
        24,
        [
            pltpu.VMEM((2, 16, LANES), F32),
            pltpu.VMEM(FIELD, F32),
            pltpu.VMEM(FIELD, F32),
            pltpu.SemaphoreType.DMA((2, 16)),
        ],
        hbm=(0, 1),
    )
    shape = velocity.shape[1:]
    return pressure.reshape(shape), residual.reshape(shape)


def solution(mesh):
    in_specs = (P(None, "fourier", None, "plane", None), P(None, "plane", None))
    out_specs = (P("fourier", None, "plane", None), P("fourier", None, "plane", None))
    return jax.shard_map(body, mesh=mesh, in_specs=in_specs, out_specs=out_specs, check_vma=False)
```

```python
import jax
import jax.numpy as jnp
import ml_dtypes
import numpy as np
from jax import lax
from jax.experimental import pallas as pl
from jax.experimental.pallas import tpu as pltpu
from jax.sharding import PartitionSpec as P

PENALTY = 10.0
BETA = 0.5
MASS_REF = 0.08
LANES = 128
F32 = jnp.float32
BF16 = jnp.bfloat16
MIB = 1 << 20
FULL = 60


def node_tables():
    nodes = np.array(
        [
            -1.0,
            -0.830223896278567,
            -0.4688487934707142,
            0.0,
            0.4688487934707142,
            0.830223896278567,
            1.0,
        ]
    )
    weights = np.array(
        [
            1.0 / 21.0,
            0.2768260473615659,
            0.4317453812098627,
            0.4876190476190476,
            0.4317453812098627,
            0.2768260473615659,
            1.0 / 21.0,
        ]
    )
    identity = np.eye(7)
    differ = nodes[:, None] - nodes[None, :] + identity
    bary = 1.0 / np.prod(differ, axis=1)
    off_diag = np.where(identity > 0.5, 0.0, bary[None, :] / bary[:, None] / differ)
    deriv = off_diag - identity * off_diag.sum(axis=1)[:, None]
    weight_diag = identity * weights[None, :]
    stiff = deriv.T @ weight_diag @ deriv
    side = np.where((np.arange(7) == 0) | (np.arange(7) == 6), 1.0, 0.0)
    rim = (side[:, None] + side[None, :]).reshape(49)
    system = np.kron(stiff, weight_diag) + np.kron(weight_diag, stiff)
    system = system + PENALTY * np.eye(49) * rim[None, :]
    system = system.astype(np.float32).astype(np.float64)
    return weights, deriv, stiff, np.linalg.inv(system)


def mode_tables(length):
    index = np.arange(length)
    wavenum = index // 2
    wavenum[1] = length // 2
    angles = 2.0 * np.pi * np.outer(index, wavenum) / length
    use_cos = (index % 2 == 0) | (index == 1)
    basis = np.where(use_cos[None, :], np.cos(angles), np.sin(angles))
    factor = np.full(length, 2.0 / length)
    factor[:2] = 1.0 / length
    forward = factor[:, None] * basis.T
    modal_diff = np.zeros((length, length))
    even = np.arange(2, length, 2)
    modal_diff[even, even + 1] = BETA * wavenum[even]
    modal_diff[even + 1, even] = -BETA * wavenum[even]
    wave_sq = (BETA * wavenum) ** 2
    return basis, forward, modal_diff, wave_sq


WEIGHTS, DERIV, STIFF, BLOCK_INV = node_tables()

ANALYSIS = np.zeros((7, 7))
SYNTHESIS = np.zeros((7, 7))
for _k in range(3):
    ANALYSIS[_k, _k] = ANALYSIS[_k, 6 - _k] = 1.0
    ANALYSIS[4 + _k, _k] = 1.0
    ANALYSIS[4 + _k, 6 - _k] = -1.0
    SYNTHESIS[_k, _k] = SYNTHESIS[6 - _k, _k] = 1.0
    SYNTHESIS[_k, 4 + _k] = 1.0
    SYNTHESIS[6 - _k, 4 + _k] = -1.0
ANALYSIS[3, 3] = SYNTHESIS[3, 3] = 1.0


def parity_form(matrix):
    return np.linalg.inv(SYNTHESIS) @ matrix @ np.linalg.inv(ANALYSIS)


DERIV_P = parity_form(DERIV)
STIFF_P = parity_form(STIFF)
_S2 = np.kron(ANALYSIS, ANALYSIS)
_R2 = np.kron(SYNTHESIS, SYNTHESIS)
BLOCK_P = np.linalg.inv(_R2) @ BLOCK_INV @ np.linalg.inv(_S2)
BLOCK_P = BLOCK_P.reshape(7, 7, 7, 7)


def analyse(v):
    return [v[0] + v[6], v[1] + v[5], v[2] + v[4], v[3], v[0] - v[6], v[1] - v[5], v[2] - v[4]]


def synthesise(g):
    return [
        g[0] + g[4],
        g[1] + g[5],
        g[2] + g[6],
        g[3],
        g[2] - g[6],
        g[1] - g[5],
        g[0] - g[4],
    ]


def mat_rows(matrix, v):
    out = []
    for row in matrix:
        acc = None
        for coef, item in zip(row, v):
            if abs(coef) > 1e-11:
                term = item * np.float32(coef)
                acc = term if acc is None else acc + term
        out.append(acc)
    return out


def derive(v):
    g = analyse(v)
    even = mat_rows(DERIV_P[:4, 4:], g[4:])
    odd = mat_rows(DERIV_P[4:, :4], g[:4])
    out = [even[k] + odd[k] for k in range(3)]
    return out + [even[3]] + [even[k] - odd[k] for k in (2, 1, 0)]


def stiffen(v):
    g = analyse(v)
    return synthesise(mat_rows(STIFF_P[:4, :4], g[:4]) + mat_rows(STIFF_P[4:, 4:], g[4:]))


def symmetric_sector(table, x, size):
    pairs = [(i, j) for i in range(size) for j in range(i, size)]
    anti = [(i, j) for i in range(size) for j in range(i + 1, size)]
    plus = [x[i][j] if i == j else x[i][j] + x[j][i] for i, j in pairs]
    minus = [x[i][j] - x[j][i] for i, j in anti]

    def sym_row(i, j):
        return [0.5 * (table[i, j, k, l] + table[i, j, l, k]) for k, l in pairs]

    def anti_row(i, j):
        return [0.5 * (table[i, j, k, l] - table[i, j, l, k]) for k, l in anti]

    top = dict(zip(pairs, mat_rows([sym_row(i, j) for i, j in pairs], plus)))
    low = dict(zip(anti, mat_rows([anti_row(i, j) for i, j in anti], minus)))
    out = [[None] * size for _ in range(size)]
    for i, j in pairs:
        if i == j:
            out[i][j] = top[i, j]
        else:
            out[i][j] = top[i, j] + low[i, j]
            out[j][i] = top[i, j] - low[i, j]
    return out


def block_solve(v):
    part = [[None] * 7 for _ in range(7)]
    for b in range(7):
        column = analyse([v[7 * a + b] for a in range(7)])
        for k in range(7):
            part[k][b] = column[k]
    part = [analyse(part[k]) for k in range(7)]
    out = [[None] * 7 for _ in range(7)]
    ev, od = slice(0, 4), slice(4, 7)
    for rows, cols in ((ev, ev), (od, od), (ev, od), (od, ev)):
        ri, ci = range(7)[rows], range(7)[cols]
        x = [[part[i][j] for j in ci] for i in ri]
        table = BLOCK_P[rows, cols, rows, cols]
        if rows == cols:
            y = symmetric_sector(table, x, len(ri))
        else:
            n = len(ri) * len(ci)
            flat = mat_rows(table.reshape(n, n), [x[i][j] for i in range(len(ri)) for j in range(len(ci))])
            y = [flat[i * len(ci) : (i + 1) * len(ci)] for i in range(len(ri))]
        for i, row in zip(ri, y):
            for j, item in zip(ci, row):
                out[i][j] = item
    out = [synthesise(out[k]) for k in range(7)]
    res = [None] * 49
    for b in range(7):
        column = synthesise([out[k][b] for k in range(7)])
        for a in range(7):
            res[7 * a + b] = column[a]
    return res


def params(limit_mib, grid=None):
    semantics = None if grid is None else ("arbitrary",) * grid
    return pltpu.CompilerParams(vmem_limit_bytes=limit_mib * MIB, dimension_semantics=semantics)


STEPS = ((0, 0), (2, 0), (1, 0), (3, 0), (2, 1), (1, 1), (3, 1), (0, 1))


PAIRS = tuple((STEPS.index((d, 0)), STEPS.index((d, 1))) for d in range(4))


def partner(me, d, flip):
    core = me % 2
    return ((me // 2 + d) % 4) * 2 + (core + flip - 2 * core * flip)


def permute(value, step):
    d, flip = STEPS[step]
    return lax.ppermute(value, "fourier", [(i, partner(i, d, flip)) for i in range(8)])


def target(me, step):
    return partner(me, *STEPS[step])


def origin(me, step):
    d, flip = STEPS[step]
    return partner(me, (4 - d) % 4, flip)


def pack_kernel(me_ref, block_ref, *out_refs):
    me = me_ref[0]
    in_ref = block_ref.reshape(8 * 392, LANES)
    rows = [target(me, s) for s in range(8)]

    def step(n, carry):
        for s in range(8):
            out_refs[s][0, n] = in_ref[pl.ds(n * 8 + rows[s], 8, stride=392), :]
        return carry

    lax.fori_loop(0, 49, step, 0, unroll=7)


def pack(me, split, x):
    return pl.pallas_call(
        pack_kernel,
        grid=(2,),
        in_specs=[
            pl.BlockSpec(memory_space=pltpu.SMEM),
            pl.BlockSpec((1, 4, 1, 2, 392, LANES), lambda p: (x, 0, p, 0, 0, 0)),
        ],
        out_specs=[pl.BlockSpec((1, 49, 8, LANES), lambda p: (p, 0, 0, 0)) for _ in range(8)],
        out_shape=[pltpu.HBM((2, 49, 8, LANES), F32) for _ in range(8)],
        compiler_params=params(FULL, 1),
        name="pack",
    )(me, split)


def transform(me, block_of, w_ref, xb, field, slope):
    core = me % 2
    for first, second in PAIRS:
        at = pl.multiple_of((origin(me, first) // 2) * 16, 16)
        for b in range(7):
            lanes = pl.ds(b * 128, 128)
            for p in range(2):
                block = jnp.concatenate([block_of(first, p, b), block_of(second, p, b)], axis=0)
                hi = block.astype(BF16)
                xb[pl.ds(at + 192 * p, 16), lanes] = hi
                xb[pl.ds(at + 192 * p + 64, 16), lanes] = (block - hi.astype(F32)).astype(BF16)
                xb[pl.ds(at + 192 * p + 128, 16), lanes] = hi
    even = jnp.dot(w_ref[core, 0], xb[0:192], preferred_element_type=F32)
    odd = jnp.dot(w_ref[core, 1], xb[192:384], preferred_element_type=F32)
    field[0:64] = even[0:64] + odd[0:64]
    field[64:128] = even[0:64] - odd[0:64]
    slope[0:64] = even[64:128] + odd[64:128]
    slope[64:128] = even[64:128] - odd[64:128]


def row_copies(sources, a, slots, sems):
    slot = a % 2
    return [
        pltpu.make_async_copy(ref.at[:, pl.ds(7 * a, 7)], slots.at[slot, i], sems.at[slot, i])
        for i, ref in enumerate(sources)
    ]


def stream_rows(sources, slots, sems, work):
    for copy in row_copies(sources, 0, slots, sems):
        copy.start()

    def step(a, carry):
        @pl.when(a < 6)
        def _():
            for copy in row_copies(sources, a + 1, slots, sems):
                copy.start()

        for copy in row_copies(sources, a, slots, sems):
            copy.wait()
        work(a)
        return carry

    lax.fori_loop(0, 7, step, 0)


BLOCK = [pl.ds(b * 128, 128) for b in range(7)]


def q_rows(t, offset=0):
    return pl.ds(pl.multiple_of(t * 8 + offset, 8), 8)


def early_kernel(*refs):
    me_ref, sources = refs[0], refs[1:17]
    met_ref, w_ref = refs[17:19]
    u, v, zu, zv, adv0, adv1, xb, slots, sems = refs[19:]
    me = me_ref[0]
    sx = met_ref[0]
    sy = met_ref[1]

    def node_row(a):
        for x, (field, slope) in enumerate(((u, zu), (v, zv))):
            transform(
                me, lambda s, p, b: slots[a % 2, 8 * x + s, p, b], w_ref, xb, field.at[a], slope.at[a]
            )

        def along_b(t, carry):
            q = q_rows(t)
            first = [u[a, q, s] for s in BLOCK]
            second = [v[a, q, s] for s in BLOCK]
            scaled = [item * sy for item in second]
            for field, out, scale in ((first, adv0, sx), (second, adv1, sy)):
                slope = derive(field)
                for b in range(7):
                    out[a, q, BLOCK[b]] = (scaled[b] * slope[b]) * scale
            for s in BLOCK:
                zu[a, q, s] = zu[a, q, s] * sx
                zv[a, q, s] = zv[a, q, s] * sy
            return carry

        lax.fori_loop(0, 16, along_b, 0)

    stream_rows(sources, slots, sems, node_row)

    def along_a(t, carry):
        q = q_rows(t)
        for s in BLOCK:
            first = [u[k, q, s] for k in range(7)]
            second = [v[k, q, s] for k in range(7)]
            scaled = [item * sx for item in first]
            for field, out, scale in ((first, adv0, sx), (second, adv1, sy)):
                slope = derive(field)
                for k in range(7):
                    out[k, q, s] = out[k, q, s] + (scaled[k] * slope[k]) * scale
            for k in range(7):
                u[k, q, s] = scaled[k]
                v[k, q, s] = second[k] * sy
        return carry

    lax.fori_loop(0, 16, along_a, 0)


def late_kernel(*refs):
    me_ref, sources = refs[0], refs[1:9]
    u, v, zu, zv, adv0, adv1 = refs[9:15]
    met_ref, w_ref, f_ref = refs[15:18]
    outs = refs[18:26]
    xb, w, zw, sum0, div, forward, db = refs[26:]
    me = me_ref[0]
    sx = met_ref[0]
    sy = met_ref[1]
    for d, (first, _) in enumerate(PAIRS):
        at = pl.ds(pl.multiple_of((target(me, first) // 2) * 16, 16), 16)
        for p in range(2):
            forward[p, d * 16 : d * 16 + 16] = f_ref[me % 2, p, 0, at]
            forward[p, 64 + d * 16 : 80 + d * 16] = f_ref[me % 2, p, 1, at]

    def node_row(a, carry):
        transform(me, lambda s, p, b: sources[s][p, 7 * a + b], w_ref, xb, w.at[a], zw)

        def along_b(t, carry):
            q = q_rows(t)
            q2 = q_rows(t, 128)
            third = [w[a, q, s] for s in BLOCK]
            slope = derive(third)
            line = []
            for b, s in enumerate(BLOCK):
                sum0[a, q, s] = adv0[a, q, s] + third[b] * zu[a, q, s]
                line.append(adv1[a, q, s] + third[b] * zv[a, q, s])
                div[a, q2, s] = v[a, q, s] * slope[b] + third[b] * zw[q, s]
            slope = derive(line)
            for b, s in enumerate(BLOCK):
                div[a, q, s] = slope[b]
            return carry

        lax.fori_loop(0, 16, along_b, 0, unroll=4)
        return carry

    lax.fori_loop(0, 7, node_row, 0)

    def along_a(t, carry):
        q = q_rows(t)
        q2 = q_rows(t, 128)
        for s in BLOCK:
            slope = derive([w[k, q, s] for k in range(7)])
            for k in range(7):
                div[k, q2, s] = div[k, q2, s] + u[k, q, s] * slope[k]
            slope = derive([sum0[k, q, s] for k in range(7)])
            for k in range(7):
                div[k, q, s] = div[k, q, s] + slope[k]
        return carry

    lax.fori_loop(0, 16, along_a, 0, unroll=2)
    area = -1.0 / (sx * sy)
    for k in range(7):
        for p in range(2):
            for i in range(2):
                one, two = div[k, 128 * i : 128 * i + 64], div[k, 128 * i + 64 : 128 * i + 128]
                block = one + two if p == 0 else one - two
                hi = block.astype(BF16)
                db[k % 2, p, 64 * i : 64 * i + 64] = hi
                db[k % 2, p, 128 + 64 * i : 192 + 64 * i] = (block - hi.astype(F32)).astype(BF16)
        for p in range(2):
            both = jnp.dot(forward[p], db[k % 2, p], preferred_element_type=F32)
            spec = both[0:64] + both[64:128]
            for b in range(7):
                scale = area * np.float32(WEIGHTS[k] * WEIGHTS[b])
                for d, pair in enumerate(PAIRS):
                    for flip, s in enumerate(pair):
                        low = 16 * d + 8 * flip
                        value = spec[low : low + 8, b * 128 : b * 128 + 128] * scale
                        outs[s][7 * k + b, 8 * p : 8 * p + 8] = value


def parity_columns(core, parity):
    return [
        16 * (2 * y + (core + flip) % 2) + 4 * g + 2 * parity + r
        for y in range(4)
        for flip in range(2)
        for g in range(4)
        for r in range(2)
    ]


def wave_tables(basis, forward, modal_diff):
    planes, modes = [], []
    for core in range(2):
        for parity in range(2):
            c = parity_columns(core, parity)
            hi, lo = split_bf16(np.concatenate([basis[:64, c], (basis @ modal_diff)[:64, c]]))
            planes.append(np.concatenate([hi, hi, lo], axis=1))
            back = np.concatenate([forward[c, :64], (modal_diff @ forward)[c, :64]], axis=1)
            hi, lo = split_bf16(back)
            modes.append(np.stack([np.concatenate([hi, hi], 1), np.concatenate([lo, 0 * lo], 1)]))
    return (
        jnp.asarray(np.stack(planes).reshape(2, 2, 128, 192)),
        jnp.asarray(np.stack(modes).reshape(2, 2, 2, 64, 256)),
    )


def split_bf16(table):
    table = table.astype(np.float32)
    hi = table.astype(ml_dtypes.bfloat16)
    return hi, (table - hi.astype(np.float32)).astype(ml_dtypes.bfloat16)


def rows_of(c, n):
    return pl.ds(pl.multiple_of(c * 392 + n * 8, 8), 8)


def metric_values(met_ref):
    sx, sy = met_ref[0], met_ref[1]
    ratio = sx / sy
    back = sy / sx
    return ratio, back, 1.0 / (sx * sy)


def inverse_divisor(ratio, back, area, wave):
    return 1.0 / (0.5 * (ratio + back) + (wave * MASS_REF) * area)


def store_rims(field, c, east_ref, west_ref):
    for b in range(7):
        east_ref[pl.ds(c * 8 + b, 1), :] = field[42 + b][7:8]
        west_ref[pl.ds(c * 8 + b, 1), :] = field[b][0:1]


def apply_operator(v, wave, ratio, back, area):
    kind = [0, 1, 2, 3, 2, 1, 0]
    sub = lax.broadcasted_iota(jnp.int32, (8, LANES), 0)
    lane = lax.broadcasted_iota(jnp.int32, (8, LANES), 1)
    w = [np.float32(WEIGHTS[k]) for k in range(4)]
    ratio_w = [ratio * w[k] for k in range(4)]
    back_w = [back * w[k] for k in range(4)]
    mass = wave * area
    diag = {}
    for i in range(4):
        for j in range(i, 4):
            rim = PENALTY * ((i == 0) + (j == 0))
            diag[i, j] = mass * np.float32(WEIGHTS[i] * WEIGHTS[j]) + np.float32(rim)
    out = [None] * 49
    for b in range(7):
        column = stiffen([v[7 * a + b] for a in range(7)])
        for a in range(7):
            key = tuple(sorted((kind[a], kind[b])))
            out[7 * a + b] = column[a] * ratio_w[kind[b]] + v[7 * a + b] * diag[key]
    for a in range(7):
        line = stiffen([v[7 * a + b] for b in range(7)])
        for b in range(7):
            out[7 * a + b] = out[7 * a + b] + line[b] * back_w[kind[a]]
    ten = np.float32(PENALTY)
    for b in range(7):
        before = jnp.where(sub == 0, 0.0, pltpu.roll(v[42 + b], 1, 0))
        after = jnp.where(sub == 7, 0.0, pltpu.roll(v[b], 7, 0))
        out[b] = out[b] - ten * before
        out[42 + b] = out[42 + b] - ten * after
    for a in range(7):
        south = jnp.where(lane == 0, 0.0, pltpu.roll(v[7 * a + 6], 1, 1))
        north = jnp.where(lane == 127, 0.0, pltpu.roll(v[7 * a], 127, 1))
        out[7 * a] = out[7 * a] - ten * south
        out[7 * a + 6] = out[7 * a + 6] - ten * north
    return out


def first_kernel(me_ref, wave_ref, *refs):
    recv, (met_ref, r_ref, p_ref, east_ref, west_ref) = refs[:8], refs[8:]
    rows = [origin(me_ref[0], s) for s in range(8)]

    def unpack(n, carry):
        for s in range(8):
            r_ref[pl.ds(n * 8 + rows[s], 16, stride=392), :] = recv[s][n]
        return carry

    lax.fori_loop(0, 49, unpack, 0, unroll=7)
    east_ref[...] = jnp.zeros_like(east_ref)
    west_ref[...] = jnp.zeros_like(west_ref)
    ratio, back, area = metric_values(met_ref)

    def step(c, carry):
        inv = inverse_divisor(ratio, back, area, wave_ref[c])
        field = block_solve([r_ref[rows_of(c, n), :] for n in range(49)])
        field = [item * inv for item in field]
        for n in range(49):
            p_ref[rows_of(c, n), :] = field[n]
        store_rims(field, c, east_ref, west_ref)
        return carry

    lax.fori_loop(0, 16, step, 0)


def rim_fix(value, kind, c, b, edge_ref):
    sub = lax.broadcasted_iota(jnp.int32, (8, LANES), 0)
    row = 0 if kind == "west" else 7
    return jnp.where(sub == row, value - np.float32(PENALTY) * edge_ref[pl.ds(c * 8 + b, 1), :], value)


def local_image_kernel(wave_ref, p_ref, met_ref, q_ref):
    ratio, back, area = metric_values(met_ref)

    def image(c, carry):
        v = [p_ref[rows_of(c, n), :] for n in range(49)]
        out = apply_operator(v, wave_ref[c], ratio, back, area)
        for n in range(49):
            q_ref[rows_of(c, n), :] = out[n]
        return carry

    lax.fori_loop(0, 16, image, 0)


def second_kernel(
    wave_ref, local_ref, met_ref, west_in, east_in, q_ref, s_ref, east_ref, west_ref
):
    east_ref[...] = jnp.zeros_like(east_ref)
    west_ref[...] = jnp.zeros_like(west_ref)
    ratio, back, area = metric_values(met_ref)

    def search(c, carry):
        inv = inverse_divisor(ratio, back, area, wave_ref[c])
        field = [local_ref[rows_of(c, n), :] for n in range(49)]
        for b in range(7):
            field[b] = rim_fix(field[b], "west", c, b, west_in)
            field[42 + b] = rim_fix(field[42 + b], "east", c, b, east_in)
        for n in range(49):
            q_ref[rows_of(c, n), :] = field[n]
        field = block_solve(field)
        field = [item * inv for item in field]
        for n in range(49):
            s_ref[rows_of(c, n), :] = field[n]
        store_rims(field, c, east_ref, west_ref)
        return carry

    lax.fori_loop(0, 16, search, 0)


def third_kernel(wave_ref, r_ref, q_ref, s_ref, met_ref, t_ref, acc_ref):
    ratio, back, area = metric_values(met_ref)

    def image(c, carry):
        v = [s_ref[rows_of(c, n), :] for n in range(49)]
        out = apply_operator(v, wave_ref[c], ratio, back, area)
        sums = [None] * 5
        for n in range(49):
            t_ref[rows_of(c, n), :] = out[n]
            q, r, t = q_ref[rows_of(c, n), :], r_ref[rows_of(c, n), :], out[n]
            for k, term in enumerate((q * q, r * q, t * q, t * t, r * t)):
                sums[k] = term if sums[k] is None else sums[k] + term
        for k in range(5):
            acc_ref[k, pl.ds(c, 1), :] = jnp.sum(sums[k], axis=0, keepdims=True)
        return carry

    lax.fori_loop(0, 16, image, 0)


def product_kernel(r_ref, q_ref, t_ref, acc_ref, west_in, east_in, dots_ref, add_ref, table_ref, sem):
    def step(c, carry):
        tq = jnp.zeros((1, LANES), F32)
        tt, rt = tq, tq
        for b in range(7):
            for n, row, edge_ref in ((b, 0, west_in), (42 + b, 7, east_in)):
                at = pl.ds(c * 392 + n * 8 + row, 1)
                change = -np.float32(PENALTY) * edge_ref[pl.ds(c * 8 + b, 1), :]
                tq = tq + change * q_ref[at, :]
                rt = rt + change * r_ref[at, :]
                tt = tt + change * (2.0 * t_ref[at, :] + change)
        for k, item in enumerate((tq, tt, rt)):
            add_ref[k, pl.ds(c, 1), :] = item
        return carry

    lax.fori_loop(0, 16, step, 0)
    lane = lax.broadcasted_iota(jnp.int32, (16, LANES), 1)
    table = jnp.zeros((16, LANES), F32)
    for k in range(5):
        total = acc_ref[k] if k < 2 else acc_ref[k] + add_ref[k - 2]
        table = jnp.where(lane == k, jnp.sum(total, axis=1, keepdims=True), table)
    for d in range(16):
        table_ref[d] = table
    copy = pltpu.make_async_copy(table_ref, dots_ref, sem)
    copy.start()
    copy.wait()


def last_kernel(
    dots_ref, r_ref, p_ref, q_ref, s_ref, t_ref, west_in, east_in,
    pres_ref, resid_ref, coef_ref, pres_buf, resid_buf, sems,
):
    total = dots_ref[0]
    for d in range(1, 16):
        total = total + dots_ref[d]
    lane = lax.broadcasted_iota(jnp.int32, (16, LANES), 1)

    def pick(k):
        return jnp.sum(jnp.where(lane == k, total, 0.0), axis=1, keepdims=True)

    qq, rq, tq, tt, rt = [pick(k) for k in range(5)]
    alpha = rq / qq
    gamma = tq / qq
    lam = (rt - gamma * rq) / (tt - gamma * tq)
    coef_ref[0] = jnp.broadcast_to(alpha - lam * gamma, (16, LANES))
    coef_ref[1] = jnp.broadcast_to(lam, (16, LANES))

    def copies(c):
        mode = 4 * ((c // 2) % 4) + 2 * (c // 8) + c % 2
        at = pl.ds(pl.multiple_of(c * 392, 8), 392)
        to = pl.ds(pl.multiple_of(mode * 392, 8), 392)
        return (
            pltpu.make_async_copy(pres_buf.at[at, :], pres_ref.at[to, :], sems.at[0, c]),
            pltpu.make_async_copy(resid_buf.at[at, :], resid_ref.at[to, :], sems.at[1, c]),
        )

    def step(c, carry):
        first = coef_ref[0, pl.ds(c, 1), :]
        second = coef_ref[1, pl.ds(c, 1), :]
        for n in range(49):
            at = rows_of(c, n)
            t = t_ref[at, :]
            if n < 7:
                t = rim_fix(t, "west", c, n, west_in)
            if n >= 42:
                t = rim_fix(t, "east", c, n - 42, east_in)
            pres_buf[at, :] = first * p_ref[at, :] + second * s_ref[at, :]
            resid_buf[at, :] = r_ref[at, :] - first * q_ref[at, :] - second * t
        for copy in copies(c):
            copy.start()
        return carry

    lax.fori_loop(0, 16, step, 0)

    def finish(c, carry):
        for copy in copies(c):
            copy.wait()
        return carry

    lax.fori_loop(0, 16, finish, 0)


FIELD = (16 * 392, LANES)
RIM = (16 * 8, LANES)


def call(kernel, name, inputs, outs, limit, scratch=(), smem=(), any_in=(), hbm=(), cost=None):
    specs = [
        pl.BlockSpec(
            memory_space=pltpu.SMEM if i in smem else pl.ANY if i in any_in else pltpu.VMEM
        )
        for i in range(len(inputs))
    ]
    out_specs = [
        pl.BlockSpec(memory_space=pltpu.HBM if i in hbm else pltpu.VMEM) for i in range(len(outs))
    ]
    return pl.pallas_call(
        kernel,
        in_specs=specs,
        out_specs=out_specs,
        out_shape=[jax.ShapeDtypeStruct(s, F32) for s in outs],
        scratch_shapes=list(scratch),
        compiler_params=params(limit),
        cost_estimate=cost and pl.CostEstimate(flops=0, bytes_accessed=cost, transcendentals=0),
        name=name,
    )(*inputs)


def body(velocity, metric):
    modes_here = velocity.shape[1]
    basis, forward, modal_diff, wave_all = mode_tables(modes_here * lax.axis_size("fourier"))
    mine = lax.axis_index("fourier")
    me = mine.astype(jnp.int32).reshape(1)
    wave_all = wave_all.reshape(-1, 4, 2, 2).transpose(0, 2, 1, 3).reshape(-1)
    wave = lax.dynamic_slice_in_dim(jnp.asarray(wave_all, F32), mine * modes_here, modes_here)
    met_row = lax.dynamic_slice_in_dim(metric, mine, 1, 1)
    to_planes, to_modes = wave_tables(basis, forward, modal_diff)

    split = pltpu.with_memory_space_constraint(
        velocity.reshape(3, 4, 2, 2, 392, LANES), pltpu.HBM
    )
    gathered = []
    for x in range(3):
        packed = pack(me, split, x)
        blocks = [packed[0]] + [permute(packed[s], s) for s in range(1, 8)]
        if x < 2:
            blocks = [pltpu.with_memory_space_constraint(item, pltpu.HBM) for item in blocks]
        gathered.append(blocks)

    plane_field = (7, 128, 896)
    early = call(
        early_kernel,
        "early",
        (me, *gathered[0], *gathered[1], met_row, to_planes),
        [plane_field] * 6,
        8,
        [
            pltpu.VMEM((384, 896), BF16),
            pltpu.VMEM((2, 16, 2, 7, 8, LANES), F32),
            pltpu.SemaphoreType.DMA((2, 16)),
        ],
        smem=(0,),
        any_in=range(1, 17),
        cost=40 * MIB,
    )
    source = call(
        late_kernel,
        "late",
        (me, *gathered[2], *early, met_row, to_planes, to_modes),
        [(49, 16, LANES)] * 8,
        22,
        [
            pltpu.VMEM((384, 896), BF16),
            pltpu.VMEM(plane_field, F32),
            pltpu.VMEM((128, 896), F32),
            pltpu.VMEM(plane_field, F32),
            pltpu.VMEM((7, 256, 896), F32),
            pltpu.VMEM((2, 128, 256), BF16),
            pltpu.VMEM((2, 2, 256, 896), BF16),
        ],
        smem=(0,),
        cost=40 * MIB,
    )
    recv = [source[0]] + [permute(source[s], s) for s in range(1, 8)]

    size = lax.axis_size("plane")
    up = [(i, i + 1) for i in range(size - 1)]
    down = [(j, i) for i, j in up]

    def exchange(east, west):
        return lax.ppermute(east, "plane", up), lax.ppermute(west, "plane", down)

    r, p1, east, west = call(
        first_kernel,
        "first",
        (me, wave, *recv, metric),
        [FIELD, FIELD, RIM, RIM],
        24,
        smem=(0, 1),
    )
    west_in, east_in = exchange(east, west)
    (local,) = call(
        local_image_kernel, "local_image", (wave, p1, metric), [FIELD], 16, smem=(0,), cost=8 * MIB
    )
    q1, s, east, west = call(
        second_kernel,
        "second",
        (wave, local, metric, west_in, east_in),
        [FIELD, FIELD, RIM, RIM],
        16,
        smem=(0,),
    )
    west_in, east_in = exchange(east, west)
    t, acc = call(
        third_kernel,
        "third",
        (wave, r, q1, s, metric),
        [FIELD, (5, 16, LANES)],
        16,
        smem=(0,),
        cost=12 * MIB,
    )
    (dots,) = call(
        product_kernel,
        "products",
        (r, q1, t, acc, west_in, east_in),
        [(16, 16, LANES)],
        16,
        [
            pltpu.VMEM((3, 16, LANES), F32),
            pltpu.VMEM((16, 16, LANES), F32),
            pltpu.SemaphoreType.DMA,
        ],
        hbm=(0,),
    )
    dots = lax.all_to_all(dots, "plane", 0, 0, tiled=True)
    pressure, residual = call(
        last_kernel,
        "last",
        (dots, r, p1, q1, s, t, west_in, east_in),
        [FIELD, FIELD],
        24,
        [
            pltpu.VMEM((2, 16, LANES), F32),
            pltpu.VMEM(FIELD, F32),
            pltpu.VMEM(FIELD, F32),
            pltpu.SemaphoreType.DMA((2, 16)),
        ],
        hbm=(0, 1),
    )
    shape = velocity.shape[1:]
    return pressure.reshape(shape), residual.reshape(shape)


def solution(mesh):
    in_specs = (P(None, "fourier", None, "plane", None), P(None, "plane", None))
    out_specs = (P("fourier", None, "plane", None), P("fourier", None, "plane", None))
    return jax.shard_map(body, mesh=mesh, in_specs=in_specs, out_specs=out_specs, check_vma=False)
```

```python
import jax
import jax.numpy as jnp
import ml_dtypes
import numpy as np
from jax import lax
from jax.experimental import pallas as pl
from jax.experimental.pallas import tpu as pltpu
from jax.sharding import PartitionSpec as P

PENALTY = 10.0
BETA = 0.5
MASS_REF = 0.08
LANES = 128
F32 = jnp.float32
BF16 = jnp.bfloat16
MIB = 1 << 20
FULL = 60


def node_tables():
    nodes = np.array(
        [
            -1.0,
            -0.830223896278567,
            -0.4688487934707142,
            0.0,
            0.4688487934707142,
            0.830223896278567,
            1.0,
        ]
    )
    weights = np.array(
        [
            1.0 / 21.0,
            0.2768260473615659,
            0.4317453812098627,
            0.4876190476190476,
            0.4317453812098627,
            0.2768260473615659,
            1.0 / 21.0,
        ]
    )
    identity = np.eye(7)
    differ = nodes[:, None] - nodes[None, :] + identity
    bary = 1.0 / np.prod(differ, axis=1)
    off_diag = np.where(identity > 0.5, 0.0, bary[None, :] / bary[:, None] / differ)
    deriv = off_diag - identity * off_diag.sum(axis=1)[:, None]
    weight_diag = identity * weights[None, :]
    stiff = deriv.T @ weight_diag @ deriv
    side = np.where((np.arange(7) == 0) | (np.arange(7) == 6), 1.0, 0.0)
    rim = (side[:, None] + side[None, :]).reshape(49)
    system = np.kron(stiff, weight_diag) + np.kron(weight_diag, stiff)
    system = system + PENALTY * np.eye(49) * rim[None, :]
    system = system.astype(np.float32).astype(np.float64)
    return weights, deriv, stiff, np.linalg.inv(system)


def mode_tables(length):
    index = np.arange(length)
    wavenum = index // 2
    wavenum[1] = length // 2
    angles = 2.0 * np.pi * np.outer(index, wavenum) / length
    use_cos = (index % 2 == 0) | (index == 1)
    basis = np.where(use_cos[None, :], np.cos(angles), np.sin(angles))
    factor = np.full(length, 2.0 / length)
    factor[:2] = 1.0 / length
    forward = factor[:, None] * basis.T
    modal_diff = np.zeros((length, length))
    even = np.arange(2, length, 2)
    modal_diff[even, even + 1] = BETA * wavenum[even]
    modal_diff[even + 1, even] = -BETA * wavenum[even]
    wave_sq = (BETA * wavenum) ** 2
    return basis, forward, modal_diff, wave_sq


WEIGHTS, DERIV, STIFF, BLOCK_INV = node_tables()

ANALYSIS = np.zeros((7, 7))
SYNTHESIS = np.zeros((7, 7))
for _k in range(3):
    ANALYSIS[_k, _k] = ANALYSIS[_k, 6 - _k] = 1.0
    ANALYSIS[4 + _k, _k] = 1.0
    ANALYSIS[4 + _k, 6 - _k] = -1.0
    SYNTHESIS[_k, _k] = SYNTHESIS[6 - _k, _k] = 1.0
    SYNTHESIS[_k, 4 + _k] = 1.0
    SYNTHESIS[6 - _k, 4 + _k] = -1.0
ANALYSIS[3, 3] = SYNTHESIS[3, 3] = 1.0


def parity_form(matrix):
    return np.linalg.inv(SYNTHESIS) @ matrix @ np.linalg.inv(ANALYSIS)


DERIV_P = parity_form(DERIV)
STIFF_P = parity_form(STIFF)
_S2 = np.kron(ANALYSIS, ANALYSIS)
_R2 = np.kron(SYNTHESIS, SYNTHESIS)
BLOCK_P = np.linalg.inv(_R2) @ BLOCK_INV @ np.linalg.inv(_S2)
BLOCK_P = BLOCK_P.reshape(7, 7, 7, 7)


def analyse(v):
    return [v[0] + v[6], v[1] + v[5], v[2] + v[4], v[3], v[0] - v[6], v[1] - v[5], v[2] - v[4]]


def synthesise(g):
    return [
        g[0] + g[4],
        g[1] + g[5],
        g[2] + g[6],
        g[3],
        g[2] - g[6],
        g[1] - g[5],
        g[0] - g[4],
    ]


def mat_rows(matrix, v):
    out = []
    for row in matrix:
        acc = None
        for coef, item in zip(row, v):
            if abs(coef) > 1e-11:
                term = item * np.float32(coef)
                acc = term if acc is None else acc + term
        out.append(acc)
    return out


def derive(v):
    g = analyse(v)
    even = mat_rows(DERIV_P[:4, 4:], g[4:])
    odd = mat_rows(DERIV_P[4:, :4], g[:4])
    out = [even[k] + odd[k] for k in range(3)]
    return out + [even[3]] + [even[k] - odd[k] for k in (2, 1, 0)]


def stiffen(v):
    g = analyse(v)
    return synthesise(mat_rows(STIFF_P[:4, :4], g[:4]) + mat_rows(STIFF_P[4:, 4:], g[4:]))


def symmetric_sector(table, x, size):
    pairs = [(i, j) for i in range(size) for j in range(i, size)]
    anti = [(i, j) for i in range(size) for j in range(i + 1, size)]
    plus = [x[i][j] if i == j else x[i][j] + x[j][i] for i, j in pairs]
    minus = [x[i][j] - x[j][i] for i, j in anti]

    def sym_row(i, j):
        return [0.5 * (table[i, j, k, l] + table[i, j, l, k]) for k, l in pairs]

    def anti_row(i, j):
        return [0.5 * (table[i, j, k, l] - table[i, j, l, k]) for k, l in anti]

    top = dict(zip(pairs, mat_rows([sym_row(i, j) for i, j in pairs], plus)))
    low = dict(zip(anti, mat_rows([anti_row(i, j) for i, j in anti], minus)))
    out = [[None] * size for _ in range(size)]
    for i, j in pairs:
        if i == j:
            out[i][j] = top[i, j]
        else:
            out[i][j] = top[i, j] + low[i, j]
            out[j][i] = top[i, j] - low[i, j]
    return out


def block_solve(v):
    part = [[None] * 7 for _ in range(7)]
    for b in range(7):
        column = analyse([v[7 * a + b] for a in range(7)])
        for k in range(7):
            part[k][b] = column[k]
    part = [analyse(part[k]) for k in range(7)]
    out = [[None] * 7 for _ in range(7)]
    ev, od = slice(0, 4), slice(4, 7)
    for rows, cols in ((ev, ev), (od, od), (ev, od), (od, ev)):
        ri, ci = range(7)[rows], range(7)[cols]
        x = [[part[i][j] for j in ci] for i in ri]
        table = BLOCK_P[rows, cols, rows, cols]
        if rows == cols:
            y = symmetric_sector(table, x, len(ri))
        else:
            n = len(ri) * len(ci)
            flat = mat_rows(table.reshape(n, n), [x[i][j] for i in range(len(ri)) for j in range(len(ci))])
            y = [flat[i * len(ci) : (i + 1) * len(ci)] for i in range(len(ri))]
        for i, row in zip(ri, y):
            for j, item in zip(ci, row):
                out[i][j] = item
    out = [synthesise(out[k]) for k in range(7)]
    res = [None] * 49
    for b in range(7):
        column = synthesise([out[k][b] for k in range(7)])
        for a in range(7):
            res[7 * a + b] = column[a]
    return res


def params(limit_mib, grid=None):
    semantics = None if grid is None else ("arbitrary",) * grid
    return pltpu.CompilerParams(vmem_limit_bytes=limit_mib * MIB, dimension_semantics=semantics)


STEPS = ((0, 0), (1, 0), (3, 0), (2, 0), (1, 1), (3, 1), (2, 1), (0, 1))


PAIRS = tuple((STEPS.index((d, 0)), STEPS.index((d, 1))) for d in range(4))


def partner(me, d, flip):
    core = me % 2
    return ((me // 2 + d) % 4) * 2 + (core + flip - 2 * core * flip)


def permute(value, step):
    d, flip = STEPS[step]
    return lax.ppermute(value, "fourier", [(i, partner(i, d, flip)) for i in range(8)])


def target(me, step):
    return partner(me, *STEPS[step])


def origin(me, step):
    d, flip = STEPS[step]
    return partner(me, (4 - d) % 4, flip)


def pack_kernel(me_ref, block_ref, *out_refs):
    me = me_ref[0]
    in_ref = block_ref.reshape(8 * 392, LANES)
    rows = [target(me, s) for s in range(8)]

    def step(n, carry):
        for s in range(8):
            out_refs[s][0, n] = in_ref[pl.ds(n * 8 + rows[s], 8, stride=392), :]
        return carry

    lax.fori_loop(0, 49, step, 0, unroll=7)


def pack(me, split, x):
    return pl.pallas_call(
        pack_kernel,
        grid=(2,),
        in_specs=[
            pl.BlockSpec(memory_space=pltpu.SMEM),
            pl.BlockSpec((1, 4, 1, 2, 392, LANES), lambda p: (x, 0, p, 0, 0, 0)),
        ],
        out_specs=[pl.BlockSpec((1, 49, 8, LANES), lambda p: (p, 0, 0, 0)) for _ in range(8)],
        out_shape=[pltpu.HBM((2, 49, 8, LANES), F32) for _ in range(8)],
        compiler_params=params(FULL, 1),
        name="pack",
    )(me, split)


def transform(me, block_of, w_ref, xb, field, slope):
    core = me % 2
    for first, second in PAIRS:
        at = pl.multiple_of((origin(me, first) // 2) * 16, 16)
        for b in range(7):
            lanes = pl.ds(b * 128, 128)
            for p in range(2):
                block = jnp.concatenate([block_of(first, p, b), block_of(second, p, b)], axis=0)
                hi = block.astype(BF16)
                xb[pl.ds(at + 192 * p, 16), lanes] = hi
                xb[pl.ds(at + 192 * p + 64, 16), lanes] = (block - hi.astype(F32)).astype(BF16)
                xb[pl.ds(at + 192 * p + 128, 16), lanes] = hi
    even = jnp.dot(w_ref[core, 0], xb[0:192], preferred_element_type=F32)
    odd = jnp.dot(w_ref[core, 1], xb[192:384], preferred_element_type=F32)
    field[0:64] = even[0:64] + odd[0:64]
    field[64:128] = even[0:64] - odd[0:64]
    slope[0:64] = even[64:128] + odd[64:128]
    slope[64:128] = even[64:128] - odd[64:128]


def row_copies(sources, a, slots, sems):
    slot = a % 2
    return [
        pltpu.make_async_copy(ref.at[:, pl.ds(7 * a, 7)], slots.at[slot, i], sems.at[slot, i])
        for i, ref in enumerate(sources)
    ]


def stream_rows(sources, slots, sems, work):
    for copy in row_copies(sources, 0, slots, sems):
        copy.start()

    def step(a, carry):
        @pl.when(a < 6)
        def _():
            for copy in row_copies(sources, a + 1, slots, sems):
                copy.start()

        for copy in row_copies(sources, a, slots, sems):
            copy.wait()
        work(a)
        return carry

    lax.fori_loop(0, 7, step, 0)


BLOCK = [pl.ds(b * 128, 128) for b in range(7)]


def q_rows(t, offset=0):
    return pl.ds(pl.multiple_of(t * 8 + offset, 8), 8)


def early_kernel(*refs):
    me_ref, sources = refs[0], refs[1:17]
    met_ref, w_ref = refs[17:19]
    u, v, zu, zv, adv0, adv1, xb, slots, sems = refs[19:]
    me = me_ref[0]
    sx = met_ref[0]
    sy = met_ref[1]

    def node_row(a):
        for x, (field, slope) in enumerate(((u, zu), (v, zv))):
            transform(
                me, lambda s, p, b: slots[a % 2, 8 * x + s, p, b], w_ref, xb, field.at[a], slope.at[a]
            )

        def along_b(t, carry):
            q = q_rows(t)
            first = [u[a, q, s] for s in BLOCK]
            second = [v[a, q, s] for s in BLOCK]
            scaled = [item * sy for item in second]
            for field, out, scale in ((first, adv0, sx), (second, adv1, sy)):
                slope = derive(field)
                for b in range(7):
                    out[a, q, BLOCK[b]] = (scaled[b] * slope[b]) * scale
            for s in BLOCK:
                zu[a, q, s] = zu[a, q, s] * sx
                zv[a, q, s] = zv[a, q, s] * sy
            return carry

        lax.fori_loop(0, 16, along_b, 0)

    stream_rows(sources, slots, sems, node_row)

    def along_a(t, carry):
        q = q_rows(t)
        for s in BLOCK:
            first = [u[k, q, s] for k in range(7)]
            second = [v[k, q, s] for k in range(7)]
            scaled = [item * sx for item in first]
            for field, out, scale in ((first, adv0, sx), (second, adv1, sy)):
                slope = derive(field)
                for k in range(7):
                    out[k, q, s] = out[k, q, s] + (scaled[k] * slope[k]) * scale
            for k in range(7):
                u[k, q, s] = scaled[k]
                v[k, q, s] = second[k] * sy
        return carry

    lax.fori_loop(0, 16, along_a, 0)


def late_kernel(*refs):
    me_ref, sources = refs[0], refs[1:9]
    u, v, zu, zv, adv0, adv1 = refs[9:15]
    met_ref, w_ref, f_ref = refs[15:18]
    outs = refs[18:26]
    xb, w, zw, sum0, div, forward, db = refs[26:]
    me = me_ref[0]
    sx = met_ref[0]
    sy = met_ref[1]
    for d, (first, _) in enumerate(PAIRS):
        at = pl.ds(pl.multiple_of((target(me, first) // 2) * 16, 16), 16)
        for p in range(2):
            forward[p, d * 16 : d * 16 + 16] = f_ref[me % 2, p, 0, at]
            forward[p, 64 + d * 16 : 80 + d * 16] = f_ref[me % 2, p, 1, at]

    def node_row(a, carry):
        transform(me, lambda s, p, b: sources[s][p, 7 * a + b], w_ref, xb, w.at[a], zw)

        def along_b(t, carry):
            q = q_rows(t)
            q2 = q_rows(t, 128)
            third = [w[a, q, s] for s in BLOCK]
            slope = derive(third)
            line = []
            for b, s in enumerate(BLOCK):
                sum0[a, q, s] = adv0[a, q, s] + third[b] * zu[a, q, s]
                line.append(adv1[a, q, s] + third[b] * zv[a, q, s])
                div[a, q2, s] = v[a, q, s] * slope[b] + third[b] * zw[q, s]
            slope = derive(line)
            for b, s in enumerate(BLOCK):
                div[a, q, s] = slope[b]
            return carry

        lax.fori_loop(0, 16, along_b, 0, unroll=4)
        return carry

    lax.fori_loop(0, 7, node_row, 0)

    def along_a(t, carry):
        q = q_rows(t)
        q2 = q_rows(t, 128)
        for s in BLOCK:
            slope = derive([w[k, q, s] for k in range(7)])
            for k in range(7):
                div[k, q2, s] = div[k, q2, s] + u[k, q, s] * slope[k]
            slope = derive([sum0[k, q, s] for k in range(7)])
            for k in range(7):
                div[k, q, s] = div[k, q, s] + slope[k]
        return carry

    lax.fori_loop(0, 16, along_a, 0, unroll=2)
    area = -1.0 / (sx * sy)
    for k in range(7):
        for p in range(2):
            for i in range(2):
                one, two = div[k, 128 * i : 128 * i + 64], div[k, 128 * i + 64 : 128 * i + 128]
                block = one + two if p == 0 else one - two
                hi = block.astype(BF16)
                db[k % 2, p, 64 * i : 64 * i + 64] = hi
                db[k % 2, p, 128 + 64 * i : 192 + 64 * i] = (block - hi.astype(F32)).astype(BF16)
        for p in range(2):
            both = jnp.dot(forward[p], db[k % 2, p], preferred_element_type=F32)
            spec = both[0:64] + both[64:128]
            for b in range(7):
                scale = area * np.float32(WEIGHTS[k] * WEIGHTS[b])
                for d, pair in enumerate(PAIRS):
                    for flip, s in enumerate(pair):
                        low = 16 * d + 8 * flip
                        value = spec[low : low + 8, b * 128 : b * 128 + 128] * scale
                        outs[s][7 * k + b, 8 * p : 8 * p + 8] = value


def parity_columns(core, parity):
    return [
        16 * (2 * y + (core + flip) % 2) + 4 * g + 2 * parity + r
        for y in range(4)
        for flip in range(2)
        for g in range(4)
        for r in range(2)
    ]


def wave_tables(basis, forward, modal_diff):
    planes, modes = [], []
    for core in range(2):
        for parity in range(2):
            c = parity_columns(core, parity)
            hi, lo = split_bf16(np.concatenate([basis[:64, c], (basis @ modal_diff)[:64, c]]))
            planes.append(np.concatenate([hi, hi, lo], axis=1))
            back = np.concatenate([forward[c, :64], (modal_diff @ forward)[c, :64]], axis=1)
            hi, lo = split_bf16(back)
            modes.append(np.stack([np.concatenate([hi, hi], 1), np.concatenate([lo, 0 * lo], 1)]))
    return (
        jnp.asarray(np.stack(planes).reshape(2, 2, 128, 192)),
        jnp.asarray(np.stack(modes).reshape(2, 2, 2, 64, 256)),
    )


def split_bf16(table):
    table = table.astype(np.float32)
    hi = table.astype(ml_dtypes.bfloat16)
    return hi, (table - hi.astype(np.float32)).astype(ml_dtypes.bfloat16)


def rows_of(c, n):
    return pl.ds(pl.multiple_of(c * 392 + n * 8, 8), 8)


def metric_values(met_ref):
    sx, sy = met_ref[0], met_ref[1]
    ratio = sx / sy
    back = sy / sx
    return ratio, back, 1.0 / (sx * sy)


def inverse_divisor(ratio, back, area, wave):
    return 1.0 / (0.5 * (ratio + back) + (wave * MASS_REF) * area)


def store_rims(field, c, east_ref, west_ref):
    for b in range(7):
        east_ref[pl.ds(c * 8 + b, 1), :] = field[42 + b][7:8]
        west_ref[pl.ds(c * 8 + b, 1), :] = field[b][0:1]


def apply_operator(v, wave, ratio, back, area):
    kind = [0, 1, 2, 3, 2, 1, 0]
    sub = lax.broadcasted_iota(jnp.int32, (8, LANES), 0)
    lane = lax.broadcasted_iota(jnp.int32, (8, LANES), 1)
    w = [np.float32(WEIGHTS[k]) for k in range(4)]
    ratio_w = [ratio * w[k] for k in range(4)]
    back_w = [back * w[k] for k in range(4)]
    mass = wave * area
    diag = {}
    for i in range(4):
        for j in range(i, 4):
            rim = PENALTY * ((i == 0) + (j == 0))
            diag[i, j] = mass * np.float32(WEIGHTS[i] * WEIGHTS[j]) + np.float32(rim)
    out = [None] * 49
    for b in range(7):
        column = stiffen([v[7 * a + b] for a in range(7)])
        for a in range(7):
            key = tuple(sorted((kind[a], kind[b])))
            out[7 * a + b] = column[a] * ratio_w[kind[b]] + v[7 * a + b] * diag[key]
    for a in range(7):
        line = stiffen([v[7 * a + b] for b in range(7)])
        for b in range(7):
            out[7 * a + b] = out[7 * a + b] + line[b] * back_w[kind[a]]
    ten = np.float32(PENALTY)
    for b in range(7):
        before = jnp.where(sub == 0, 0.0, pltpu.roll(v[42 + b], 1, 0))
        after = jnp.where(sub == 7, 0.0, pltpu.roll(v[b], 7, 0))
        out[b] = out[b] - ten * before
        out[42 + b] = out[42 + b] - ten * after
    for a in range(7):
        south = jnp.where(lane == 0, 0.0, pltpu.roll(v[7 * a + 6], 1, 1))
        north = jnp.where(lane == 127, 0.0, pltpu.roll(v[7 * a], 127, 1))
        out[7 * a] = out[7 * a] - ten * south
        out[7 * a + 6] = out[7 * a + 6] - ten * north
    return out


def first_kernel(me_ref, wave_ref, *refs):
    recv, (met_ref, r_ref, p_ref, east_ref, west_ref) = refs[:8], refs[8:]
    rows = [origin(me_ref[0], s) for s in range(8)]

    def unpack(n, carry):
        for s in range(8):
            r_ref[pl.ds(n * 8 + rows[s], 16, stride=392), :] = recv[s][n]
        return carry

    lax.fori_loop(0, 49, unpack, 0, unroll=7)
    east_ref[...] = jnp.zeros_like(east_ref)
    west_ref[...] = jnp.zeros_like(west_ref)
    ratio, back, area = metric_values(met_ref)

    def step(c, carry):
        inv = inverse_divisor(ratio, back, area, wave_ref[c])
        field = block_solve([r_ref[rows_of(c, n), :] for n in range(49)])
        field = [item * inv for item in field]
        for n in range(49):
            p_ref[rows_of(c, n), :] = field[n]
        store_rims(field, c, east_ref, west_ref)
        return carry

    lax.fori_loop(0, 16, step, 0, unroll=2)


def rim_fix(value, kind, c, b, edge_ref):
    sub = lax.broadcasted_iota(jnp.int32, (8, LANES), 0)
    row = 0 if kind == "west" else 7
    return jnp.where(sub == row, value - np.float32(PENALTY) * edge_ref[pl.ds(c * 8 + b, 1), :], value)


def local_image_kernel(wave_ref, p_ref, met_ref, q_ref):
    ratio, back, area = metric_values(met_ref)

    def image(c, carry):
        v = [p_ref[rows_of(c, n), :] for n in range(49)]
        out = apply_operator(v, wave_ref[c], ratio, back, area)
        for n in range(49):
            q_ref[rows_of(c, n), :] = out[n]
        return carry

    lax.fori_loop(0, 16, image, 0, unroll=2)


def second_kernel(
    wave_ref, local_ref, met_ref, west_in, east_in, q_ref, s_ref, east_ref, west_ref
):
    east_ref[...] = jnp.zeros_like(east_ref)
    west_ref[...] = jnp.zeros_like(west_ref)
    ratio, back, area = metric_values(met_ref)

    def search(c, carry):
        inv = inverse_divisor(ratio, back, area, wave_ref[c])
        field = [local_ref[rows_of(c, n), :] for n in range(49)]
        for b in range(7):
            field[b] = rim_fix(field[b], "west", c, b, west_in)
            field[42 + b] = rim_fix(field[42 + b], "east", c, b, east_in)
        for n in range(49):
            q_ref[rows_of(c, n), :] = field[n]
        field = block_solve(field)
        field = [item * inv for item in field]
        for n in range(49):
            s_ref[rows_of(c, n), :] = field[n]
        store_rims(field, c, east_ref, west_ref)
        return carry

    lax.fori_loop(0, 16, search, 0, unroll=2)


def third_kernel(wave_ref, r_ref, q_ref, s_ref, met_ref, t_ref, acc_ref):
    ratio, back, area = metric_values(met_ref)

    def image(c, carry):
        v = [s_ref[rows_of(c, n), :] for n in range(49)]
        out = apply_operator(v, wave_ref[c], ratio, back, area)
        sums = [None] * 5
        for n in range(49):
            t_ref[rows_of(c, n), :] = out[n]
            q, r, t = q_ref[rows_of(c, n), :], r_ref[rows_of(c, n), :], out[n]
            for k, term in enumerate((q * q, r * q, t * q, t * t, r * t)):
                sums[k] = term if sums[k] is None else sums[k] + term
        for k in range(5):
            acc_ref[k, pl.ds(c, 1), :] = jnp.sum(sums[k], axis=0, keepdims=True)
        return carry

    lax.fori_loop(0, 16, image, 0, unroll=2)


def product_kernel(r_ref, q_ref, t_ref, acc_ref, west_in, east_in, dots_ref, add_ref, table_ref, sem):
    def step(c, carry):
        tq = jnp.zeros((1, LANES), F32)
        tt, rt = tq, tq
        for b in range(7):
            for n, row, edge_ref in ((b, 0, west_in), (42 + b, 7, east_in)):
                at = pl.ds(c * 392 + n * 8 + row, 1)
                change = -np.float32(PENALTY) * edge_ref[pl.ds(c * 8 + b, 1), :]
                tq = tq + change * q_ref[at, :]
                rt = rt + change * r_ref[at, :]
                tt = tt + change * (2.0 * t_ref[at, :] + change)
        for k, item in enumerate((tq, tt, rt)):
            add_ref[k, pl.ds(c, 1), :] = item
        return carry

    lax.fori_loop(0, 16, step, 0)
    lane = lax.broadcasted_iota(jnp.int32, (16, LANES), 1)
    table = jnp.zeros((16, LANES), F32)
    for k in range(5):
        total = acc_ref[k] if k < 2 else acc_ref[k] + add_ref[k - 2]
        table = jnp.where(lane == k, jnp.sum(total, axis=1, keepdims=True), table)
    for d in range(16):
        table_ref[d] = table
    copy = pltpu.make_async_copy(table_ref, dots_ref, sem)
    copy.start()
    copy.wait()


def last_kernel(
    dots_ref, r_ref, p_ref, q_ref, s_ref, t_ref, west_in, east_in,
    pres_ref, resid_ref, coef_ref, pres_buf, resid_buf, sems,
):
    total = dots_ref[0]
    for d in range(1, 16):
        total = total + dots_ref[d]
    lane = lax.broadcasted_iota(jnp.int32, (16, LANES), 1)

    def pick(k):
        return jnp.sum(jnp.where(lane == k, total, 0.0), axis=1, keepdims=True)

    qq, rq, tq, tt, rt = [pick(k) for k in range(5)]
    alpha = rq / qq
    gamma = tq / qq
    lam = (rt - gamma * rq) / (tt - gamma * tq)
    coef_ref[0] = jnp.broadcast_to(alpha - lam * gamma, (16, LANES))
    coef_ref[1] = jnp.broadcast_to(lam, (16, LANES))

    def copies(c):
        mode = 4 * ((c // 2) % 4) + 2 * (c // 8) + c % 2
        at = pl.ds(pl.multiple_of(c * 392, 8), 392)
        to = pl.ds(pl.multiple_of(mode * 392, 8), 392)
        return (
            pltpu.make_async_copy(pres_buf.at[at, :], pres_ref.at[to, :], sems.at[0, c]),
            pltpu.make_async_copy(resid_buf.at[at, :], resid_ref.at[to, :], sems.at[1, c]),
        )

    def step(c, carry):
        first = coef_ref[0, pl.ds(c, 1), :]
        second = coef_ref[1, pl.ds(c, 1), :]
        for n in range(49):
            at = rows_of(c, n)
            t = t_ref[at, :]
            if n < 7:
                t = rim_fix(t, "west", c, n, west_in)
            if n >= 42:
                t = rim_fix(t, "east", c, n - 42, east_in)
            pres_buf[at, :] = first * p_ref[at, :] + second * s_ref[at, :]
            resid_buf[at, :] = r_ref[at, :] - first * q_ref[at, :] - second * t
        for copy in copies(c):
            copy.start()
        return carry

    lax.fori_loop(0, 16, step, 0)

    def finish(c, carry):
        for copy in copies(c):
            copy.wait()
        return carry

    lax.fori_loop(0, 16, finish, 0)


FIELD = (16 * 392, LANES)
RIM = (16 * 8, LANES)


def call(kernel, name, inputs, outs, limit, scratch=(), smem=(), any_in=(), hbm=(), cost=None):
    specs = [
        pl.BlockSpec(
            memory_space=pltpu.SMEM if i in smem else pl.ANY if i in any_in else pltpu.VMEM
        )
        for i in range(len(inputs))
    ]
    out_specs = [
        pl.BlockSpec(memory_space=pltpu.HBM if i in hbm else pltpu.VMEM) for i in range(len(outs))
    ]
    return pl.pallas_call(
        kernel,
        in_specs=specs,
        out_specs=out_specs,
        out_shape=[jax.ShapeDtypeStruct(s, F32) for s in outs],
        scratch_shapes=list(scratch),
        compiler_params=params(limit),
        cost_estimate=cost and pl.CostEstimate(flops=0, bytes_accessed=cost, transcendentals=0),
        name=name,
    )(*inputs)


def body(velocity, metric):
    modes_here = velocity.shape[1]
    basis, forward, modal_diff, wave_all = mode_tables(modes_here * lax.axis_size("fourier"))
    mine = lax.axis_index("fourier")
    me = mine.astype(jnp.int32).reshape(1)
    wave_all = wave_all.reshape(-1, 4, 2, 2).transpose(0, 2, 1, 3).reshape(-1)
    wave = lax.dynamic_slice_in_dim(jnp.asarray(wave_all, F32), mine * modes_here, modes_here)
    met_row = lax.dynamic_slice_in_dim(metric, mine, 1, 1)
    to_planes, to_modes = wave_tables(basis, forward, modal_diff)

    split = pltpu.with_memory_space_constraint(
        velocity.reshape(3, 4, 2, 2, 392, LANES), pltpu.HBM
    )
    gathered = []
    for x in range(3):
        packed = pack(me, split, x)
        blocks = [packed[0]] + [permute(packed[s], s) for s in range(1, 8)]
        if x < 2:
            blocks = [pltpu.with_memory_space_constraint(item, pltpu.HBM) for item in blocks]
        gathered.append(blocks)

    plane_field = (7, 128, 896)
    early = call(
        early_kernel,
        "early",
        (me, *gathered[0], *gathered[1], met_row, to_planes),
        [plane_field] * 6,
        8,
        [
            pltpu.VMEM((384, 896), BF16),
            pltpu.VMEM((2, 16, 2, 7, 8, LANES), F32),
            pltpu.SemaphoreType.DMA((2, 16)),
        ],
        smem=(0,),
        any_in=range(1, 17),
        cost=40 * MIB,
    )
    source = call(
        late_kernel,
        "late",
        (me, *gathered[2], *early, met_row, to_planes, to_modes),
        [(49, 16, LANES)] * 8,
        22,
        [
            pltpu.VMEM((384, 896), BF16),
            pltpu.VMEM(plane_field, F32),
            pltpu.VMEM((128, 896), F32),
            pltpu.VMEM(plane_field, F32),
            pltpu.VMEM((7, 256, 896), F32),
            pltpu.VMEM((2, 128, 256), BF16),
            pltpu.VMEM((2, 2, 256, 896), BF16),
        ],
        smem=(0,),
        cost=40 * MIB,
    )
    recv = [source[0]] + [permute(source[s], s) for s in range(1, 8)]

    size = lax.axis_size("plane")
    up = [(i, i + 1) for i in range(size - 1)]
    down = [(j, i) for i, j in up]

    def exchange(east, west):
        return lax.ppermute(east, "plane", up), lax.ppermute(west, "plane", down)

    r, p1, east, west = call(
        first_kernel,
        "first",
        (me, wave, *recv, metric),
        [FIELD, FIELD, RIM, RIM],
        24,
        smem=(0, 1),
    )
    west_in, east_in = exchange(east, west)
    (local,) = call(
        local_image_kernel, "local_image", (wave, p1, metric), [FIELD], 16, smem=(0,), cost=8 * MIB
    )
    q1, s, east, west = call(
        second_kernel,
        "second",
        (wave, local, metric, west_in, east_in),
        [FIELD, FIELD, RIM, RIM],
        16,
        smem=(0,),
    )
    west_in, east_in = exchange(east, west)
    t, acc = call(
        third_kernel,
        "third",
        (wave, r, q1, s, metric),
        [FIELD, (5, 16, LANES)],
        16,
        smem=(0,),
        cost=12 * MIB,
    )
    (dots,) = call(
        product_kernel,
        "products",
        (r, q1, t, acc, west_in, east_in),
        [(16, 16, LANES)],
        16,
        [
            pltpu.VMEM((3, 16, LANES), F32),
            pltpu.VMEM((16, 16, LANES), F32),
            pltpu.SemaphoreType.DMA,
        ],
        hbm=(0,),
    )
    dots = lax.all_to_all(dots, "plane", 0, 0, tiled=True)
    pressure, residual = call(
        last_kernel,
        "last",
        (dots, r, p1, q1, s, t, west_in, east_in),
        [FIELD, FIELD],
        24,
        [
            pltpu.VMEM((2, 16, LANES), F32),
            pltpu.VMEM(FIELD, F32),
            pltpu.VMEM(FIELD, F32),
            pltpu.SemaphoreType.DMA((2, 16)),
        ],
        hbm=(0, 1),
    )
    shape = velocity.shape[1:]
    return pressure.reshape(shape), residual.reshape(shape)


def solution(mesh):
    in_specs = (P(None, "fourier", None, "plane", None), P(None, "plane", None))
    out_specs = (P("fourier", None, "plane", None), P("fourier", None, "plane", None))
    return jax.shard_map(body, mesh=mesh, in_specs=in_specs, out_specs=out_specs, check_vma=False)
```
